256 devices in a mesh: tm: 16 (over z_hi, y, core), head: 4 (over x), branch: 4 (over z_lo).
Axes of the slice: x: 4, y: 4, z: 8 (z_hi: 2, z_lo: 4; z = z_hi * 4 + z_lo), core: 2. Of those that a mesh axis runs over, the one named last changes fastest.
Arguments:
- queries: bfloat16 [4, 16, 512, 20, 128], P('branch', 'tm', 'head'), may hold values from -8 to 8
- keys: bfloat16 [4, 16, 512, 20, 128], P('branch', 'tm', 'head'), may hold values from -5 to 5
- values: bfloat16 [4, 16, 512, 20, 128], P('branch', 'tm', 'head'), may hold values from -6 to 6
- ctx_keys: bfloat16 [16, 512, 20, 128], P('tm', ('head', 'branch')), may hold values from -5 to 5
- ctx_values: bfloat16 [16, 512, 20, 128], P('tm', ('head', 'branch')), may hold values from -6 to 6
- hidden: bfloat16 [4, 16, 512, 5120], P('branch', 'tm', 'head'), may hold values from -6 to 6
- out_weight: bfloat16 [2560, 5120], P('head'), may hold values from -0.5 to 0.5
- gates: float32 [16, 5120], replicated, may hold values from 0.5 to 2
- levels: int32 [16], replicated, may hold values from 0 to 15
- span_mask: int32 [16, 16], replicated, may hold values from 0 to 1, as said below
- prefix: int32 [1], replicated, may hold values from 1 to 15
Outputs:
- updated: bfloat16 [4, 16, 512, 5120], P('branch', 'tm', 'head')
The draws below stay inside these ranges and needn't reach their ends.
Inputs may be any that keep to these rules, and one draw needn't show every extreme that they name: `span_mask`: 1 on the diagonal and in the first column, 0 above the diagonal.
All inputs are finite; a program needn't handle non-finite values.
Results may differ from the reference program's by a relative error of at most 0.01.
Values may be sent and summed in bfloat16 or wider, within the bound.
A program may use at most 256 MiB of HBM per device.

```python
import math
import jax
import jax.numpy as jnp
from jax import lax

D = 5120
H = 20
HD = 128
TOK = 512
LEVELS = 16
SPANS = 16
BRANCHES = 4
HEAD_GROUP = 5


def draw_keys(key, part):
    base_draw = jax.random.normal(jax.random.fold_in(key, 21), (BRANCHES, SPANS, TOK, H, HD), jnp.float32)
    return jnp.clip(base_draw, -5.0, 5.0).astype(jnp.bfloat16)


def draw_queries(key, part):
    base_draw = jax.random.normal(jax.random.fold_in(key, 31), (BRANCHES, SPANS, TOK, H, HD), jnp.float32)
    base_draw = 2.0 * base_draw
    return jnp.clip(base_draw, -8.0, 8.0).astype(jnp.bfloat16)


def draw_span_mask(key, part):
    coins = jax.random.randint(jax.random.fold_in(key, 41), (SPANS, SPANS), 0, 4)
    row_ids = jnp.arange(SPANS, dtype=jnp.int32)[:, None]
    col_ids = jnp.arange(SPANS, dtype=jnp.int32)[None, :]
    keep_cell = (col_ids < row_ids) & (coins > 0) | (col_ids == row_ids) | (col_ids == 0)
    return keep_cell.astype(jnp.int32)


def set_ends(result, rng, low, high):
    place = [jax.random.randint(jax.random.fold_in(rng, axis), (), 0, length) for axis, length in enumerate(result.shape)]
    widest = result.shape.index(max(result.shape))
    beside = place[:widest] + [(place[widest] + 1) % result.shape[widest]] + place[widest + 1:]
    return result.at[tuple(place)].set(low).at[tuple(beside)].set(high)


def steps_of(key, extent, shards, least, high):
    loudness, own = 1.0, jax.random.fold_in(key, 6)
    for axis_at, blocks in shards:
        heights = jnp.exp(jax.random.uniform(jax.random.fold_in(own, axis_at), (blocks,), jnp.float32, least / len(shards), high / len(shards)))
        loudness = loudness * jnp.repeat(heights, extent[axis_at] // blocks).reshape([-1 if axis == axis_at else 1 for axis in range(len(extent))])
    return loudness


def scatter_about(rng, dims, spread, reach, pieces=(), held_as=jnp.bfloat16):
    entries = jax.random.normal(rng, dims, jnp.float32) * spread
    if len(pieces) > 0:
        entries = steps_of(rng, dims, pieces, -0.22, 0.18) * entries
    return jnp.clip(entries, min=-reach, max=reach).astype(held_as)


def setup_inputs(seed: int = 0) -> dict:
    splits = jax.random.split(jax.random.key(seed), 12)
    return {
        "queries": draw_queries(jax.random.fold_in(splits[11], 71), 0),
        "keys": draw_keys(jax.random.fold_in(splits[11], 71), 0),
        "values": scatter_about(splits[2], (BRANCHES, SPANS, TOK, H, HD), 1.0, 6.0, ((0, 4), (1, 16), (2, 4))),
        "ctx_keys": scatter_about(splits[3], (SPANS, TOK, H, HD), 1.0, 5.0, ((0, 16), (1, 16))),
        "ctx_values": scatter_about(splits[4], (SPANS, TOK, H, HD), 1.0, 6.0, ((0, 16), (1, 16))),
        "hidden": scatter_about(splits[5], (BRANCHES, SPANS, TOK, D), 1.0, 6.0, ((0, 4), (1, 16), (2, 4))),
        "out_weight": scatter_about(splits[6], (H * HD, D), HD ** -0.5, 0.5, ((0, 4),)),
        "gates": jnp.clip(jax.random.uniform(splits[7], (LEVELS, D), jnp.float32, 0.5, 2.0), 0.5, 2.0),
        "levels": set_ends(jax.random.randint(splits[8], (SPANS,), 0, LEVELS), jax.random.fold_in(splits[8], 1), 0, LEVELS - 1).astype(jnp.int32),
        "span_mask": draw_span_mask(jax.random.fold_in(splits[11], 71), 0),
        "prefix": jax.random.randint(splits[10], (1,), 1, SPANS).astype(jnp.int32),
    }


NEG_BIG = -1e+30

def reference(queries, keys, values, ctx_keys, ctx_values, hidden, out_weight, gates, levels, span_mask, prefix):
    score_scale = 1.0 / math.sqrt(HD)
    use_context = jnp.arange(SPANS, dtype=jnp.int32) < prefix[0]
    weight_groups = out_weight.reshape(H // HEAD_GROUP, HEAD_GROUP, HD, D).astype(jnp.float32)

    def one_slot(slot_index):
        branch_index = slot_index // SPANS
        span_index = slot_index % SPANS
        branch_keys = lax.dynamic_index_in_dim(keys, branch_index, 0, keepdims=False)
        branch_values = lax.dynamic_index_in_dim(values, branch_index, 0, keepdims=False)
        slot_keys = jnp.where(use_context[:, None, None, None], ctx_keys, branch_keys).reshape(SPANS * TOK, H, HD)
        slot_values = jnp.where(use_context[:, None, None, None], ctx_values, branch_values).reshape(SPANS * TOK, H, HD)
        mask_row = lax.dynamic_index_in_dim(span_mask, span_index, 0, keepdims=False)
        visible = jnp.repeat(mask_row > 0, TOK)
        branch_queries = lax.dynamic_index_in_dim(queries, branch_index, 0, keepdims=False)
        span_queries = lax.dynamic_index_in_dim(branch_queries, span_index, 0, keepdims=False)

        def one_head(head_index):
            head_q = lax.dynamic_index_in_dim(span_queries, head_index, 1, keepdims=False)
            head_k = lax.dynamic_index_in_dim(slot_keys, head_index, 1, keepdims=False)
            head_v = lax.dynamic_index_in_dim(slot_values, head_index, 1, keepdims=False)
            scores = jnp.dot(head_q, head_k.T, preferred_element_type=jnp.float32) * score_scale
            row_max = lax.optimization_barrier(jnp.max(jnp.where(visible[None, :], scores, NEG_BIG), axis=1))
            exp_terms = jnp.where(visible[None, :], jnp.exp(scores - row_max[:, None]), 0.0)
            denominator = lax.optimization_barrier(jnp.sum(exp_terms, axis=1))
            summed = jnp.dot(exp_terms.astype(jnp.bfloat16), head_v, preferred_element_type=jnp.float32)
            return (summed / denominator[:, None]).astype(jnp.bfloat16)
        attended = lax.map(one_head, jnp.arange(H, dtype=jnp.int32))
        grouped = attended.reshape(H // HEAD_GROUP, HEAD_GROUP, TOK, HD).astype(jnp.float32)
        partial_value = jnp.einsum('gaqd,gadn->gqn', grouped, weight_groups).astype(jnp.bfloat16)
        partial_value = lax.optimization_barrier(partial_value)
        projected = lax.optimization_barrier(jnp.sum(partial_value.astype(jnp.float32), axis=0))
        level_now = lax.dynamic_index_in_dim(levels, span_index, 0, keepdims=False)
        gate_row = lax.dynamic_index_in_dim(gates, level_now, 0, keepdims=False)
        branch_hidden = lax.dynamic_index_in_dim(hidden, branch_index, 0, keepdims=False)
        span_hidden = lax.dynamic_index_in_dim(branch_hidden, span_index, 0, keepdims=False)
        return (span_hidden.astype(jnp.float32) + gate_row[None, :] * projected).astype(jnp.bfloat16)
    updated = lax.map(one_slot, jnp.arange(BRANCHES * SPANS, dtype=jnp.int32))
    return updated.reshape(BRANCHES, SPANS, TOK, D)
```

```python
import math

import jax
import jax.numpy as jnp
from jax import lax
from jax.experimental import pallas as pl
from jax.experimental.pallas import tpu as pltpu
from jax.sharding import PartitionSpec as P

MESH = pl.DeviceIdType.MESH
SPANS = 16
TOK = 512
HD = 128
GROUP = 5
LOW = -1e30
EXP_SCALE = math.log2(math.e) / math.sqrt(HD)


def remote(src, dst, send_sem, recv_sem, where):
    return pltpu.make_async_remote_copy(
        src_ref=src,
        dst_ref=dst,
        send_sem=send_sem,
        recv_sem=recv_sem,
        device_id=where,
        device_id_type=MESH,
    )


def attend_kernel(q_ref, kv_ref, mask_ref, out_ref, kvbuf, acc, mref, lref, send, recv, local):
    span = lax.axis_index("tm")
    zhi = span // 8
    y = (span % 8) // 2
    core = span % 2
    sibling = span + 1 - 2 * core

    def at_y(step):
        return zhi * 8 + ((y + step) % 4) * 2 + core

    barrier = pltpu.get_barrier_semaphore()
    for step in (1, 2, 3):
        pl.semaphore_signal(barrier, inc=1, device_id={"tm": at_y(step)}, device_id_type=MESH)
    pl.semaphore_signal(barrier, inc=1, device_id={"tm": (span + 8) % 16}, device_id_type=MESH)
    pl.semaphore_signal(barrier, inc=1, device_id={"tm": sibling}, device_id_type=MESH)

    own_copies = [
        pltpu.make_async_copy(kv_ref.at[h], kvbuf.at[h, span], local.at[h]) for h in range(GROUP)
    ]
    for copy in own_copies:
        copy.start()
    pl.semaphore_wait(barrier, 5)

    def item(h, c, slot, where):
        return remote(kvbuf.at[h, c], kvbuf.at[h, c], send.at[h, slot], recv.at[h, c], where)

    def transfers(h):
        own = [
            ((y + step) % 4 > y, item(h, span, step - 1, {"tm": at_y(step)})) for step in (1, 2, 3)
        ]
        own.append((zhi == 0, item(h, span, 3, {"tm": (span + 8) % 16})))
        own.append((core == 0, item(h, span, 4, {"tm": sibling})))
        far = (span + 8) % 16
        across = [
            (zhi == 1, item(h, far, 4 + step, {"tm": at_y(step)})) for step in (1, 2, 3)
        ]
        across.append((zhi == 1, item(h, far, 8, {"tm": sibling})))
        plane = [
            (((y + step) % 4 < y), at_y(step), item(h, at_y(step), 8 + step, {"tm": sibling}))
            for step in (1, 2, 3)
        ]
        below = [
            ((zhi == 1), at_y(step) % 8, item(h, at_y(step) % 8, 11 + step, {"tm": sibling}))
            for step in (1, 2, 3)
        ]
        return own, across, plane, below

    def send_own(h):
        own = transfers(h)[0]
        for cond, copy in own:
            pl.when(cond)(copy.start)

    def send_across(h):
        across = transfers(h)[1]

        @pl.when(zhi == 1)
        def _():
            across[0][1].wait_recv()
            for _, copy in across:
                copy.start()

    def send_sibling(h):
        _, _, plane, below = transfers(h)
        for cond, _, copy in plane + below:

            @pl.when(cond)
            def _():
                copy.wait_recv()
                copy.start()

    def finish(h):
        own, across, plane, below = transfers(h)
        for cond, copy in own + across:
            pl.when(cond)(copy.wait_send)
        for cond, _, copy in plane + below:
            pl.when(cond)(copy.wait_send)

    def compute(h):
        acc[...] = jnp.zeros_like(acc)
        mref[...] = jnp.full_like(mref, LOW)
        lref[...] = jnp.zeros_like(lref)

        def block(c, _):
            @pl.when(c % 2 != core)
            def _():
                item(h, c, 0, {"tm": sibling}).wait_recv()

            allowed = mask_ref[span, c].astype(jnp.float32)
            s = lax.dot_general(
                kvbuf[h, c, 0], q_ref[h], (((1,), (1,)), ((), ())), preferred_element_type=jnp.float32
            )
            top = jnp.max(s, axis=0, keepdims=True) * allowed + (1.0 - allowed) * LOW
            old = mref[...]
            new = jnp.maximum(old, top)
            p = jnp.exp2((s - (new - (1.0 - allowed) * (2.0 * LOW))) * EXP_SCALE)
            fade = jnp.exp2((old - new) * EXP_SCALE)
            mref[...] = new
            lref[...] = lref[...] * fade + jnp.sum(p, axis=0, keepdims=True)
            acc[...] = acc[...] * fade + lax.dot_general(
                kvbuf[h, c, 1],
                p.astype(jnp.bfloat16),
                (((0,), (0,)), ((), ())),
                preferred_element_type=jnp.float32,
            )
            return 0

        lax.fori_loop(0, span + 1, block, 0)
        out_ref[h] = (acc[...] / lref[...]).T.astype(jnp.bfloat16)

    for h in range(GROUP):
        own_copies[h].wait()
        if h < 2:
            send_own(h)
    send_across(0)
    send_sibling(0)

    def per_head(h, _):
        @pl.when(h + 1 < GROUP)
        def _():
            send_across(h + 1)

        @pl.when(h + 2 < GROUP)
        def _():
            send_own(h + 2)

        compute(h)

        @pl.when(h + 1 < GROUP)
        def _():
            send_sibling(h + 1)

        return 0

    lax.fori_loop(0, GROUP, per_head, 0)

    def per_head_end(h, _):
        finish(h)
        return 0

    lax.fori_loop(0, GROUP, per_head_end, 0)


def attend(q, kv, mask):
    vmem = pl.BlockSpec(memory_space=pltpu.VMEM)
    return pl.pallas_call(
        attend_kernel,
        out_shape=jax.ShapeDtypeStruct((GROUP, TOK, HD), jnp.bfloat16),
        in_specs=[vmem, pl.BlockSpec(memory_space=pl.ANY), pl.BlockSpec(memory_space=pltpu.SMEM)],
        out_specs=vmem,
        scratch_shapes=[
            pltpu.VMEM((GROUP, SPANS, 2, TOK, HD), jnp.bfloat16),
            pltpu.VMEM((HD, TOK), jnp.float32),
            pltpu.VMEM((1, TOK), jnp.float32),
            pltpu.VMEM((1, TOK), jnp.float32),
            pltpu.SemaphoreType.DMA((GROUP, 16)),
            pltpu.SemaphoreType.DMA((GROUP, SPANS)),
            pltpu.SemaphoreType.DMA((GROUP,)),
        ],
        compiler_params=pltpu.CompilerParams(
            collective_id=0, has_side_effects=True, vmem_limit_bytes=48 * 2**20
        ),
        cost_estimate=pl.CostEstimate(
            flops=4 * GROUP * TOK * TOK * SPANS * HD,
            bytes_accessed=4 * 2**20,
            transcendentals=GROUP * TOK * TOK * SPANS,
        ),
    )(q, kv, mask)


def body(
    queries,
    keys,
    values,
    ctx_keys,
    ctx_values,
    hidden,
    out_weight,
    gates,
    levels,
    span_mask,
    prefix,
):
    span_index = lax.axis_index("tm")
    q, k, v = (x[0, 0].transpose(1, 0, 2) for x in (queries, keys, values))
    ctx = jnp.stack([ctx_keys[0].transpose(1, 0, 2), ctx_values[0].transpose(1, 0, 2)], axis=1)
    ctx = lax.all_gather(ctx, "branch", axis=2, tiled=True)
    slot = jnp.where(span_index < prefix[0], ctx, jnp.stack([k, v], axis=1))
    slot = lax.all_to_all(slot, "head", split_axis=0, concat_axis=2, tiled=True)
    q = lax.all_to_all(q, "head", split_axis=0, concat_axis=1, tiled=True)
    attended = attend(q, slot, span_mask)
    weight_heads = out_weight.reshape(GROUP, HD, out_weight.shape[1])
    projected = lax.psum_scatter(
        jnp.einsum(
            "hqd,hdn->qn", attended, weight_heads, preferred_element_type=jnp.float32
        ).astype(jnp.bfloat16),
        "head",
        scatter_dimension=0,
        tiled=True,
    ).astype(jnp.float32)
    level_now = lax.dynamic_index_in_dim(levels, span_index, 0, keepdims=False)
    gate_row = lax.dynamic_index_in_dim(gates, level_now, 0, keepdims=False)
    mixed_rows = hidden[0, 0].astype(jnp.float32) + gate_row[None, :] * projected
    return mixed_rows.astype(jnp.bfloat16)[None, None]


def solution(mesh):
    return jax.shard_map(
        body,
        mesh=mesh,
        in_specs=(
            P("branch", "tm", "head", None, None),
            P("branch", "tm", "head", None, None),
            P("branch", "tm", "head", None, None),
            P("tm", ("head", "branch"), None, None),
            P("tm", ("head", "branch"), None, None),
            P("branch", "tm", "head", None),
            P("head", None),
            P(),
            P(),
            P(),
            P(),
        ),
        out_specs=P("branch", "tm", "head", None),
        check_vma=False,
    )
```

```python
import math

import jax
import jax.numpy as jnp
from jax import lax
from jax.experimental import pallas as pl
from jax.experimental.pallas import tpu as pltpu
from jax.sharding import PartitionSpec as P

MESH = pl.DeviceIdType.MESH
SPANS = 16
TOK = 512
PART = 128
CHUNK = 32
HD = 128
GROUP = 5
WIDTH = 5120
GATHERED = 3584
DIRECT = WIDTH - GATHERED
TILE = 512
LOW = -1e30
EXP_SCALE = math.log2(math.e) / math.sqrt(HD)


def remote(src, dst, send_sem, recv_sem, where):
    return pltpu.make_async_remote_copy(
        src_ref=src,
        dst_ref=dst,
        send_sem=send_sem,
        recv_sem=recv_sem,
        device_id=where,
        device_id_type=MESH,
    )


def sublayer_kernel(
    q_ref,
    k_ref,
    v_ref,
    ck_ref,
    cv_ref,
    hidden_ref,
    w_ref,
    gate_ref,
    mask_ref,
    prefix_ref,
    out_ref,
    kvbuf,
    qbuf,
    ctxbuf,
    wbuf,
    wdirect,
    hbuf,
    attloc,
    attbuf,
    psend,
    precv,
    outacc,
    acc,
    mref,
    lref,
    kv_send,
    kv_recv,
    in_send,
    in_recv,
    ctx_send,
    ctx_recv,
    w_send,
    w_recv,
    att_send,
    att_recv,
    part_send,
    part_recv,
    local,
):
    span = lax.axis_index("tm")
    x = lax.axis_index("head")
    b = lax.axis_index("branch")
    zhi = span // 8
    y = (span % 8) // 2
    core = span % 2
    sibling = {"tm": span + 1 - 2 * core}
    across = {"tm": (span + 8) % 16}

    def at_y(step):
        return zhi * 8 + ((y + step) % 4) * 2 + core

    def at_x(step):
        return (x + step) % 4

    def rows(index, size):
        return pl.ds(pl.multiple_of(index * size, size), size)

    own_rows = rows(x, PART)

    own = pl.ds(GROUP * x, GROUP)
    home = [
        pltpu.make_async_copy(ck_ref.at[own], ctxbuf.at[:, 0, x, rows(b, CHUNK)], local.at[0]),
        pltpu.make_async_copy(cv_ref.at[own], ctxbuf.at[:, 1, x, rows(b, CHUNK)], local.at[1]),
        pltpu.make_async_copy(k_ref.at[own], kvbuf.at[:, span, 0, own_rows], local.at[2]),
        pltpu.make_async_copy(v_ref.at[own], kvbuf.at[:, span, 1, own_rows], local.at[3]),
        pltpu.make_async_copy(q_ref.at[own], qbuf.at[:, own_rows], local.at[4]),
    ]
    late = [
        pltpu.make_async_copy(w_ref.at[:, :, pl.ds(GATHERED, DIRECT)], wdirect, local.at[5]),
        pltpu.make_async_copy(w_ref.at[:, :, pl.ds(0, GATHERED)], wbuf.at[:, x], local.at[6]),
        pltpu.make_async_copy(hidden_ref, hbuf, local.at[7]),
    ]
    for copy in home:
        copy.start()

    barrier = pltpu.get_barrier_semaphore()
    partners = [sibling, across]
    for step in (1, 2, 3):
        partners += [{"tm": at_y(step)}, {"head": at_x(step)}, {"branch": (b + step) % 4}]
    for where in partners:
        pl.semaphore_signal(barrier, inc=1, device_id=where, device_id_type=MESH)
    pl.semaphore_wait(barrier, len(partners))

    def entry(h, step, kind):
        g = at_x(step)
        row = GROUP * g + h
        src, dst = (
            (lambda: (ck_ref.at[row], ctxbuf.at[h, 0, x, rows(b, CHUNK)])),
            (lambda: (cv_ref.at[row], ctxbuf.at[h, 1, x, rows(b, CHUNK)])),
            (lambda: (k_ref.at[row], kvbuf.at[h, span, 0, own_rows])),
            (lambda: (v_ref.at[row], kvbuf.at[h, span, 1, own_rows])),
            (lambda: (q_ref.at[row], qbuf.at[h, own_rows])),
        )[kind]()
        return remote(
            src, dst, in_send.at[h, step - 1, kind], in_recv.at[h, step - 1, kind], {"head": g}
        )

    def entry_start(h, kinds):
        for kind in kinds:
            for step in (1, 2, 3):
                entry(h, step, kind).start()

    def entry_wait(h, kinds):
        for kind in kinds:
            for step in (1, 2, 3):
                entry(h, step, kind).wait_recv()

    def chunk(h, step):
        part = ctxbuf.at[h, :, :, rows(b, CHUNK)]
        return remote(
            part,
            part,
            ctx_send.at[h, step - 1],
            ctx_recv.at[h, step - 1],
            {"branch": (b + step) % 4},
        )

    def spread_context(h):
        entry_wait(h, (0, 1))
        for step in (1, 2, 3):
            chunk(h, step).start()

    def item(h, c, slot, where):
        return remote(kvbuf.at[h, c], kvbuf.at[h, c], kv_send.at[h, slot], kv_recv.at[h, c], where)

    def own_items(h):
        for step in (1, 2, 3):
            yield (y + step) % 4 > y, item(h, span, step - 1, {"tm": at_y(step)})
        yield zhi == 0, item(h, span, 3, across)
        yield core == 0, item(h, span, 4, sibling)

    def across_items(h):
        c = (span + 8) % 16
        for step in (1, 2, 3):
            yield zhi == 1, item(h, c, 4 + step, {"tm": at_y(step)})
        yield zhi == 1, item(h, c, 8, sibling)

    def passed_items(h):
        for step in (1, 2, 3):
            yield (y + step) % 4 < y, item(h, at_y(step), 8 + step, sibling)
        for step in (1, 2, 3):
            yield zhi == 1, item(h, at_y(step) % 8, 11 + step, sibling)

    def send_own(h):
        for step in (1, 2, 3):
            chunk(h, step).wait_recv()
        entry_wait(h, (2, 3))
        use_context = prefix_ref[0] > span
        kvbuf[h, span] = jnp.where(
            use_context, ctxbuf[h].reshape(2, TOK, HD), kvbuf[h, span]
        )
        for cond, copy in own_items(h):
            pl.when(cond)(copy.start)

    def send_across(h):
        @pl.when(zhi == 1)
        def _():
            item(h, (span + 8) % 16, 8, sibling).wait_recv()

        for cond, copy in across_items(h):
            pl.when(cond)(copy.start)

    def send_sibling(h):
        for cond, copy in passed_items(h):

            @pl.when(cond)
            def _():
                copy.wait_recv()
                copy.start()

    half = 64 * core

    def block_of_weight(h, g, start, size, slot, where, src=None):
        place = wbuf.at[h, g, pl.ds(pl.multiple_of(start, 32), size)]
        return remote(
            place if src is None else src, place, w_send.at[h, slot], w_recv.at[h, slot], where
        )

    def weight_near(h, slot):
        src = w_ref.at[h, pl.ds(pl.multiple_of(half, 64), 64), pl.ds(0, GATHERED)]
        return block_of_weight(h, x, half, 64, slot, {"head": at_x((1, 3)[slot])}, src)

    def weight_far(h, slot):
        g, to = ((at_x(3), at_x(1)), (at_x(1), at_x(3)))[slot - 2]
        return block_of_weight(h, g, half + 32 * (slot - 2), 32, slot, {"head": to})

    def weight_pass(h, slot):
        if slot == 4:
            return block_of_weight(h, at_x(3), half, 64, slot, sibling)
        if slot == 5:
            return block_of_weight(h, at_x(1), half, 64, slot, sibling)
        return block_of_weight(h, at_x(2), half + 32 * (slot - 6), 32, slot, sibling)

    def start_weight(h):
        for slot in (0, 1):
            weight_near(h, slot).start()

    def relay_weight(h):
        for slot in (0, 1):
            weight_near(h, slot).wait_recv()
            weight_far(h, 2 + slot).start()
            weight_pass(h, 4 + slot).start()

    def pass_weight(h):
        for slot in (2, 3):
            weight_far(h, slot).wait_recv()
            weight_pass(h, 4 + slot).start()

    def wait_weight(h):
        for slot in (4, 5, 6, 7):
            weight_pass(h, slot).wait_recv()

    def features(h, step):
        g = at_x(step)
        return remote(
            attloc.at[h, rows(g, PART)],
            attbuf.at[h, x],
            att_send.at[h, step - 1],
            att_recv.at[h, step - 1],
            {"head": g},
        )

    def partial_sum(step):
        return remote(
            psend.at[step - 1],
            precv.at[step - 1],
            part_send.at[step - 1],
            part_recv.at[step - 1],
            {"head": at_x(step)},
        )

    def compute(h):
        for step in (1, 2, 3):
            entry(h, step, 4).wait_recv()
        acc[...] = jnp.zeros_like(acc)
        mref[...] = jnp.full_like(mref, LOW)
        lref[...] = jnp.zeros_like(lref)

        def block(c, _):
            @pl.when(c % 2 != core)
            def _():
                item(h, c, 0, sibling).wait_recv()

            allowed = mask_ref[span, c].astype(jnp.float32)
            s = lax.dot_general(
                kvbuf[h, c, 0], qbuf[h], (((1,), (1,)), ((), ())), preferred_element_type=jnp.float32
            )
            top = jnp.max(s, axis=0, keepdims=True) * allowed + (1.0 - allowed) * LOW
            old = mref[...]
            new = jnp.maximum(old, top)
            p = jnp.exp2((s - (new - (1.0 - allowed) * (2.0 * LOW))) * EXP_SCALE)
            fade = jnp.exp2((old - new) * EXP_SCALE)
            mref[...] = new
            lref[...] = lref[...] * fade + jnp.sum(p, axis=0, keepdims=True)
            acc[...] = acc[...] * fade + lax.dot_general(
                kvbuf[h, c, 1],
                p.astype(jnp.bfloat16),
                (((0,), (0,)), ((), ())),
                preferred_element_type=jnp.float32,
            )
            return 0

        lax.fori_loop(0, span + 1, block, 0)
        attloc[h] = (acc[...] / lref[...]).T.astype(jnp.bfloat16)
        for step in (1, 2, 3):
            features(h, step).start()
        attbuf[h, x] = attloc[h, own_rows]

    def for_heads(function):
        def step(h, _):
            function(h)
            return 0

        lax.fori_loop(0, GROUP, step, 0)

    for_heads(lambda h: entry_start(h, (0, 1)))
    for_heads(lambda h: entry_start(h, (2, 3, 4)))
    for copy in late:
        copy.start()
    for copy in home:
        copy.wait()
    for_heads(spread_context)
    send_own(0)
    start_weight(0)
    send_own(1)
    start_weight(1)
    send_across(0)
    send_sibling(0)

    def per_head(h, _):
        @pl.when(h + 1 < GROUP)
        def _():
            send_across(h + 1)

        @pl.when(h + 2 < GROUP)
        def _():
            send_own(h + 2)
            start_weight(h + 2)

        compute(h)

        @pl.when(h + 1 < GROUP)
        def _():
            send_sibling(h + 1)

        @pl.when(h >= 1)
        def _():
            relay_weight(h - 1)

        @pl.when(h >= 2)
        def _():
            pass_weight(h - 2)

        return 0

    lax.fori_loop(0, GROUP, per_head, 0)
    relay_weight(GROUP - 1)

    late[0].wait()

    def partial_of(step):
        here = rows(at_x(step), PART)
        group = jnp.concatenate([attloc[h, here] for h in range(GROUP)], axis=1)
        for n in range(DIRECT // TILE):
            cols = slice(n * TILE, (n + 1) * TILE)
            value = jnp.dot(
                group,
                wdirect[:, :, cols].reshape(GROUP * HD, TILE),
                preferred_element_type=jnp.float32,
            )
            if step:
                psend[step - 1, :, cols] = value.astype(jnp.bfloat16)
            else:
                outacc[:, GATHERED + n * TILE : GATHERED + (n + 1) * TILE] = value

    for step in (2, 1, 3):
        partial_of(step)
        partial_sum(step).start()
    partial_of(0)
    pass_weight(GROUP - 2)
    late[1].wait()
    outacc[:, :GATHERED] = jnp.zeros((PART, GATHERED), jnp.float32)

    def project(h):
        wait_weight(h)
        for step in (1, 2, 3):
            features(h, step).wait_recv()
        group = jnp.concatenate([attbuf[h, g] for g in range(4)], axis=1)
        for n in range(GATHERED // TILE):
            cols = slice(n * TILE, (n + 1) * TILE)
            outacc[:, cols] += jnp.dot(
                group,
                wbuf[h, :, :, cols].reshape(4 * HD, TILE),
                preferred_element_type=jnp.float32,
            )

    def project_early(h, _):
        project(h)
        return 0

    lax.fori_loop(0, GROUP - 1, project_early, 0)
    pass_weight(GROUP - 1)
    project(GROUP - 1)
    late[2].wait()

    def finish(cols, projected):
        out_ref[:, cols] = (
            hbuf[:, cols].astype(jnp.float32) + gate_ref[:, cols] * projected
        ).astype(jnp.bfloat16)

    for n in range(GATHERED // TILE):
        cols = slice(n * TILE, (n + 1) * TILE)
        finish(cols, outacc[:, cols])
    for step in (1, 2, 3):
        partial_sum(step).wait_recv()
    for n in range(DIRECT // TILE):
        cols = slice(GATHERED + n * TILE, GATHERED + (n + 1) * TILE)
        there = slice(n * TILE, (n + 1) * TILE)
        total = outacc[:, cols]
        for step in (1, 2, 3):
            total += precv[step - 1, :, there].astype(jnp.float32)
        finish(cols, total)

    def sent(h):
        for step in (1, 2, 3):
            for kind in range(5):
                entry(h, step, kind).wait_send()
            chunk(h, step).wait_send()
            features(h, step).wait_send()
        for slot in (0, 1):
            weight_near(h, slot).wait_send()
        for slot in (2, 3):
            weight_far(h, slot).wait_send()
        for slot in (4, 5, 6, 7):
            weight_pass(h, slot).wait_send()
        for items in (own_items, across_items, passed_items):
            for cond, copy in items(h):
                pl.when(cond)(copy.wait_send)

    for_heads(sent)
    for step in (1, 2, 3):
        partial_sum(step).wait_send()


def sublayer(q, k, v, ck, cv, hidden, weight, gate, mask, prefix):
    hbm = pl.BlockSpec(memory_space=pl.ANY)
    vmem = pl.BlockSpec(memory_space=pltpu.VMEM)
    smem = pl.BlockSpec(memory_space=pltpu.SMEM)
    bf16, f32, dma = jnp.bfloat16, jnp.float32, pltpu.SemaphoreType.DMA
    return pl.pallas_call(
        sublayer_kernel,
        out_shape=jax.ShapeDtypeStruct((PART, WIDTH), bf16),
        in_specs=[hbm] * 7 + [vmem, smem, smem],
        out_specs=vmem,
        scratch_shapes=[
            pltpu.VMEM((GROUP, SPANS, 2, TOK, HD), bf16),
            pltpu.VMEM((GROUP, TOK, HD), bf16),
            pltpu.VMEM((GROUP, 2, 4, PART, HD), bf16),
            pltpu.VMEM((GROUP, 4, HD, GATHERED), bf16),
            pltpu.VMEM((GROUP, HD, DIRECT), bf16),
            pltpu.VMEM((PART, WIDTH), bf16),
            pltpu.VMEM((GROUP, TOK, HD), bf16),
            pltpu.VMEM((GROUP, 4, PART, HD), bf16),
            pltpu.VMEM((3, PART, DIRECT), bf16),
            pltpu.VMEM((3, PART, DIRECT), bf16),
            pltpu.VMEM((PART, WIDTH), f32),
            pltpu.VMEM((HD, TOK), f32),
            pltpu.VMEM((1, TOK), f32),
            pltpu.VMEM((1, TOK), f32),
            dma((GROUP, 16)),
            dma((GROUP, SPANS)),
            dma((GROUP, 3, 5)),
            dma((GROUP, 3, 5)),
            dma((GROUP, 3)),
            dma((GROUP, 3)),
            dma((GROUP, 8)),
            dma((GROUP, 8)),
            dma((GROUP, 3)),
            dma((GROUP, 3)),
            dma((3,)),
            dma((3,)),
            dma((8,)),
        ],
        compiler_params=pltpu.CompilerParams(
            collective_id=0, has_side_effects=True, vmem_limit_bytes=60 * 2**20
        ),
    )(q, k, v, ck, cv, hidden, weight, gate, mask, prefix)


def body(
    queries,
    keys,
    values,
    ctx_keys,
    ctx_values,
    hidden,
    out_weight,
    gates,
    levels,
    span_mask,
    prefix,
):
    span_index = lax.axis_index("tm")
    q, k, v = (a[0, 0].transpose(1, 0, 2) for a in (queries, keys, values))
    ck, cv = (a[0].transpose(1, 0, 2) for a in (ctx_keys, ctx_values))
    level_now = lax.dynamic_index_in_dim(levels, span_index, 0, keepdims=False)
    gate_row = lax.dynamic_index_in_dim(gates, level_now, 0, keepdims=True)
    weight = out_weight.reshape(GROUP, HD, WIDTH)
    updated = sublayer(q, k, v, ck, cv, hidden[0, 0], weight, gate_row, span_mask, prefix)
    return updated[None, None]


def solution(mesh):
    return jax.shard_map(
        body,
        mesh=mesh,
        in_specs=(
            P("branch", "tm", "head", None, None),
            P("branch", "tm", "head", None, None),
            P("branch", "tm", "head", None, None),
            P("tm", ("head", "branch"), None, None),
            P("tm", ("head", "branch"), None, None),
            P("branch", "tm", "head", None),
            P("head", None),
            P(),
            P(),
            P(),
            P(),
        ),
        out_specs=P("branch", "tm", "head", None),
        check_vma=False,
    )
```

```python
import math

import jax
import jax.numpy as jnp
from jax import lax
from jax.experimental import pallas as pl
from jax.experimental.pallas import tpu as pltpu
from jax.sharding import PartitionSpec as P

MESH = pl.DeviceIdType.MESH
SPANS = 16
TOK = 512
PART = 128
CHUNK = 32
HD = 128
GROUP = 5
WIDTH = 5120
GATHERED = 3584
DIRECT = WIDTH - GATHERED
TILE = 512
LOW = -1e30
EXP_SCALE = math.log2(math.e) / math.sqrt(HD)


def remote(src, dst, send_sem, recv_sem, where):
    return pltpu.make_async_remote_copy(
        src_ref=src,
        dst_ref=dst,
        send_sem=send_sem,
        recv_sem=recv_sem,
        device_id=where,
        device_id_type=MESH,
    )


def sublayer_kernel(
    q_ref,
    k_ref,
    v_ref,
    ck_ref,
    cv_ref,
    hidden_ref,
    w_ref,
    gate_ref,
    mask_ref,
    prefix_ref,
    out_ref,
    kvbuf,
    qbuf,
    ctxbuf,
    wbuf,
    wdirect,
    hbuf,
    attloc,
    attbuf,
    psend,
    precv,
    outacc,
    acc,
    mref,
    lref,
    kv_send,
    kv_recv,
    in_send,
    in_recv,
    ctx_send,
    ctx_recv,
    w_send,
    w_recv,
    att_send,
    att_recv,
    part_send,
    part_recv,
    local,
):
    span = lax.axis_index("tm")
    x = lax.axis_index("head")
    b = lax.axis_index("branch")
    zhi = span // 8
    y = (span % 8) // 2
    core = span % 2
    sibling = {"tm": span + 1 - 2 * core}
    across = {"tm": (span + 8) % 16}

    def at_y(step):
        return zhi * 8 + ((y + step) % 4) * 2 + core

    def at_x(step):
        return (x + step) % 4

    def rows(index, size):
        return pl.ds(pl.multiple_of(index * size, size), size)

    own_rows = rows(x, PART)

    own = pl.ds(GROUP * x, GROUP)
    home = [
        pltpu.make_async_copy(ck_ref.at[own], ctxbuf.at[:, 0, x, rows(b, CHUNK)], local.at[0]),
        pltpu.make_async_copy(cv_ref.at[own], ctxbuf.at[:, 1, x, rows(b, CHUNK)], local.at[1]),
        pltpu.make_async_copy(k_ref.at[own], kvbuf.at[:, span, 0, own_rows], local.at[2]),
        pltpu.make_async_copy(v_ref.at[own], kvbuf.at[:, span, 1, own_rows], local.at[3]),
        pltpu.make_async_copy(q_ref.at[own], qbuf.at[:, own_rows], local.at[4]),
    ]
    late = [
        pltpu.make_async_copy(w_ref.at[:, :, pl.ds(GATHERED, DIRECT)], wdirect, local.at[5]),
        pltpu.make_async_copy(w_ref.at[:, :, pl.ds(0, GATHERED)], wbuf.at[:, x], local.at[6]),
        pltpu.make_async_copy(hidden_ref, hbuf, local.at[7]),
    ]
    for copy in home:
        copy.start()

    barrier = pltpu.get_barrier_semaphore()
    partners = [sibling, across]
    for step in (1, 2, 3):
        partners += [{"tm": at_y(step)}, {"head": at_x(step)}, {"branch": (b + step) % 4}]
    for where in partners:
        pl.semaphore_signal(barrier, inc=1, device_id=where, device_id_type=MESH)
    pl.semaphore_wait(barrier, len(partners))

    def entry(h, step, kind):
        g = at_x(step)
        row = GROUP * g + h
        src, dst = (
            (lambda: (ck_ref.at[row], ctxbuf.at[h, 0, x, rows(b, CHUNK)])),
            (lambda: (cv_ref.at[row], ctxbuf.at[h, 1, x, rows(b, CHUNK)])),
            (lambda: (k_ref.at[row], kvbuf.at[h, span, 0, own_rows])),
            (lambda: (v_ref.at[row], kvbuf.at[h, span, 1, own_rows])),
            (lambda: (q_ref.at[row], qbuf.at[h, own_rows])),
        )[kind]()
        return remote(
            src, dst, in_send.at[h, step - 1, kind], in_recv.at[h, step - 1, kind], {"head": g}
        )

    def entry_start(h, kinds):
        for kind in kinds:
            for step in (1, 2, 3):
                entry(h, step, kind).start()

    def entry_wait(h, kinds):
        for kind in kinds:
            for step in (1, 2, 3):
                entry(h, step, kind).wait_recv()

    def chunk(h, step):
        part = ctxbuf.at[h, :, :, rows(b, CHUNK)]
        return remote(
            part,
            part,
            ctx_send.at[h, step - 1],
            ctx_recv.at[h, step - 1],
            {"branch": (b + step) % 4},
        )

    def spread_context(h):
        entry_wait(h, (0, 1))
        for step in (1, 2, 3):
            chunk(h, step).start()

    def item(h, c, slot, where):
        return remote(kvbuf.at[h, c], kvbuf.at[h, c], kv_send.at[h, slot], kv_recv.at[h, c], where)

    left, right = {"tm": at_y(3)}, {"tm": at_y(1)}
    upper = zhi == 1

    def own_items(h):
        yield y < 3, item(h, span, 0, right)
        yield y == 0, item(h, span, 1, left)
        yield zhi == 0, item(h, span, 2, across)
        yield core == 0, item(h, span, 3, sibling)

    def across_items(h):
        c = (span + 8) % 16
        yield upper, item(h, c, 4, right)
        yield upper, item(h, c, 5, left)
        yield upper, item(h, c, 6, sibling)

    def near_arrivals(h):
        yield y > 0, item(h, at_y(3), 7, sibling)
        yield y == 3, item(h, at_y(1), 8, sibling)
        yield upper, item(h, at_y(3) % 8, 9, sibling)
        yield upper, item(h, at_y(1) % 8, 10, sibling)

    def near_items(h):
        yield from near_arrivals(h)
        yield (y == 1) | (y == 2), item(h, at_y(3), 11, right)
        yield upper, item(h, at_y(1) % 8, 12, left)

    def far_items(h):
        yield y >= 2, item(h, at_y(2), 13, sibling)
        yield upper, item(h, at_y(2) % 8, 14, sibling)

    def send_own(h):
        for step in (1, 2, 3):
            chunk(h, step).wait_recv()
        entry_wait(h, (2, 3))
        use_context = prefix_ref[0] > span
        kvbuf[h, span] = jnp.where(
            use_context, ctxbuf[h].reshape(2, TOK, HD), kvbuf[h, span]
        )
        for cond, copy in own_items(h):
            pl.when(cond)(copy.start)

    def send_across(h):
        @pl.when(zhi == 1)
        def _():
            item(h, (span + 8) % 16, 6, sibling).wait_recv()

        for cond, copy in across_items(h):
            pl.when(cond)(copy.start)

    def send_near(h):
        for cond, copy in near_arrivals(h):
            pl.when(cond)(copy.wait_recv)
        for cond, copy in reversed(list(near_items(h))):
            pl.when(cond)(copy.start)

    def send_far(h):
        for cond, copy in far_items(h):
            pl.when(cond)(copy.wait_recv)
            pl.when(cond)(copy.start)

    half = 64 * core

    def block_of_weight(h, g, start, size, slot, where, src=None):
        place = wbuf.at[h, g, pl.ds(pl.multiple_of(start, 32), size)]
        return remote(
            place if src is None else src, place, w_send.at[h, slot], w_recv.at[h, slot], where
        )

    def weight_near(h, slot):
        src = w_ref.at[h, pl.ds(pl.multiple_of(half, 64), 64), pl.ds(0, GATHERED)]
        return block_of_weight(h, x, half, 64, slot, {"head": at_x((1, 3)[slot])}, src)

    def weight_far(h, slot):
        g, to = ((at_x(3), at_x(1)), (at_x(1), at_x(3)))[slot - 2]
        return block_of_weight(h, g, half + 32 * (slot - 2), 32, slot, {"head": to})

    def weight_pass(h, slot):
        if slot == 4:
            return block_of_weight(h, at_x(3), half, 64, slot, sibling)
        if slot == 5:
            return block_of_weight(h, at_x(1), half, 64, slot, sibling)
        return block_of_weight(h, at_x(2), half + 32 * (slot - 6), 32, slot, sibling)

    def start_weight(h):
        for slot in (0, 1):
            weight_near(h, slot).start()

    def relay_weight(h):
        for slot in (0, 1):
            weight_near(h, slot).wait_recv()
            weight_far(h, 2 + slot).start()
            weight_pass(h, 4 + slot).start()

    def pass_weight(h):
        for slot in (2, 3):
            weight_far(h, slot).wait_recv()
            weight_pass(h, 4 + slot).start()

    def wait_weight(h):
        for slot in (4, 5, 6, 7):
            weight_pass(h, slot).wait_recv()

    def features(h, step):
        g = at_x(step)
        return remote(
            attloc.at[h, rows(g, PART)],
            attbuf.at[h, x],
            att_send.at[h, step - 1],
            att_recv.at[h, step - 1],
            {"head": g},
        )

    def partial_sum(step):
        return remote(
            psend.at[step - 1],
            precv.at[step - 1],
            part_send.at[step - 1],
            part_recv.at[step - 1],
            {"head": at_x(step)},
        )

    def compute(h):
        for step in (1, 2, 3):
            entry(h, step, 4).wait_recv()
        acc[...] = jnp.zeros_like(acc)
        mref[...] = jnp.full_like(mref, LOW)
        lref[...] = jnp.zeros_like(lref)

        def block(c):
            allowed = mask_ref[span, c].astype(jnp.float32)
            s = lax.dot_general(
                kvbuf[h, c, 0], qbuf[h], (((1,), (1,)), ((), ())), preferred_element_type=jnp.float32
            )
            top = jnp.max(s, axis=0, keepdims=True) * allowed + (1.0 - allowed) * LOW
            old = mref[...]
            new = jnp.maximum(old, top)
            p = jnp.exp2((s - (new - (1.0 - allowed) * (2.0 * LOW))) * EXP_SCALE)
            fade = jnp.exp2((old - new) * EXP_SCALE)
            mref[...] = new
            lref[...] = lref[...] * fade + jnp.sum(p, axis=0, keepdims=True)
            acc[...] = acc[...] * fade + lax.dot_general(
                kvbuf[h, c, 1],
                p.astype(jnp.bfloat16),
                (((0,), (0,)), ((), ())),
                preferred_element_type=jnp.float32,
            )

        def visit(i, _):
            j = i // 4
            same = (i // 2) % 2 == 0
            turn = i % 2
            step = j + j // 2 - 2 * (j // 3)
            there = (y + step) % 4
            c = jnp.where(same, zhi, 0) * 8 + there * 2 + (core + turn) % 2
            before = (there < y) | ((step == 0) & ((turn == 0) | (core == 1)))
            seen = (same & before) | (~same & upper)

            @pl.when(seen & (turn == 1))
            def _():
                item(h, c, 0, sibling).wait_recv()

            @pl.when(seen)
            def _():
                block(c)

            return 0

        lax.fori_loop(0, 12, visit, 0)
        send_far(h)
        lax.fori_loop(12, 16, visit, 0)
        attloc[h] = (acc[...] / lref[...]).T.astype(jnp.bfloat16)
        for step in (1, 2, 3):
            features(h, step).start()
        attbuf[h, x] = attloc[h, own_rows]

    def for_heads(function):
        def step(h, _):
            function(h)
            return 0

        lax.fori_loop(0, GROUP, step, 0)

    for_heads(lambda h: entry_start(h, (0, 1)))
    for_heads(lambda h: entry_start(h, (2, 3, 4)))
    for copy in late:
        copy.start()
    for copy in home:
        copy.wait()
    for_heads(spread_context)
    send_own(0)
    start_weight(0)
    send_own(1)
    start_weight(1)
    send_across(0)
    send_own(2)
    send_near(0)
    send_across(1)

    def per_head(h, _):
        @pl.when(h + 1 < GROUP)
        def _():
            send_near(h + 1)

        @pl.when(h + 2 < GROUP)
        def _():
            send_across(h + 2)
            start_weight(h + 2)

        @pl.when(h + 3 < GROUP)
        def _():
            send_own(h + 3)

        compute(h)

        @pl.when(h >= 1)
        def _():
            relay_weight(h - 1)

        @pl.when(h >= 2)
        def _():
            pass_weight(h - 2)

        return 0

    lax.fori_loop(0, GROUP, per_head, 0)
    relay_weight(GROUP - 1)

    late[0].wait()

    def partial_of(step):
        here = rows(at_x(step), PART)
        group = jnp.concatenate([attloc[h, here] for h in range(GROUP)], axis=1)
        for n in range(DIRECT // TILE):
            cols = slice(n * TILE, (n + 1) * TILE)
            value = jnp.dot(
                group,
                wdirect[:, :, cols].reshape(GROUP * HD, TILE),
                preferred_element_type=jnp.float32,
            )
            if step:
                psend[step - 1, :, cols] = value.astype(jnp.bfloat16)
            else:
                outacc[:, GATHERED + n * TILE : GATHERED + (n + 1) * TILE] = value

    for step in (2, 1, 3):
        partial_of(step)
        partial_sum(step).start()
    partial_of(0)
    pass_weight(GROUP - 2)
    late[1].wait()
    outacc[:, :GATHERED] = jnp.zeros((PART, GATHERED), jnp.float32)

    def project(h):
        wait_weight(h)
        for step in (1, 2, 3):
            features(h, step).wait_recv()
        group = jnp.concatenate([attbuf[h, g] for g in range(4)], axis=1)
        for n in range(GATHERED // TILE):
            cols = slice(n * TILE, (n + 1) * TILE)
            outacc[:, cols] += jnp.dot(
                group,
                wbuf[h, :, :, cols].reshape(4 * HD, TILE),
                preferred_element_type=jnp.float32,
            )

    def project_early(h, _):
        project(h)
        return 0

    lax.fori_loop(0, GROUP - 1, project_early, 0)
    pass_weight(GROUP - 1)
    project(GROUP - 1)
    late[2].wait()

    def finish(cols, projected):
        out_ref[:, cols] = (
            hbuf[:, cols].astype(jnp.float32) + gate_ref[:, cols] * projected
        ).astype(jnp.bfloat16)

    for n in range(GATHERED // TILE):
        cols = slice(n * TILE, (n + 1) * TILE)
        finish(cols, outacc[:, cols])
    for step in (1, 2, 3):
        partial_sum(step).wait_recv()
    for n in range(DIRECT // TILE):
        cols = slice(GATHERED + n * TILE, GATHERED + (n + 1) * TILE)
        there = slice(n * TILE, (n + 1) * TILE)
        total = outacc[:, cols]
        for step in (1, 2, 3):
            total += precv[step - 1, :, there].astype(jnp.float32)
        finish(cols, total)

    def sent(h):
        for step in (1, 2, 3):
            for kind in range(5):
                entry(h, step, kind).wait_send()
            chunk(h, step).wait_send()
            features(h, step).wait_send()
        for slot in (0, 1):
            weight_near(h, slot).wait_send()
        for slot in (2, 3):
            weight_far(h, slot).wait_send()
        for slot in (4, 5, 6, 7):
            weight_pass(h, slot).wait_send()
        for items in (own_items, across_items, near_items, far_items):
            for cond, copy in items(h):
                pl.when(cond)(copy.wait_send)

    for_heads(sent)
    for step in (1, 2, 3):
        partial_sum(step).wait_send()


def sublayer(q, k, v, ck, cv, hidden, weight, gate, mask, prefix):
    hbm = pl.BlockSpec(memory_space=pl.ANY)
    vmem = pl.BlockSpec(memory_space=pltpu.VMEM)
    smem = pl.BlockSpec(memory_space=pltpu.SMEM)
    bf16, f32, dma = jnp.bfloat16, jnp.float32, pltpu.SemaphoreType.DMA
    return pl.pallas_call(
        sublayer_kernel,
        out_shape=jax.ShapeDtypeStruct((PART, WIDTH), bf16),
        in_specs=[hbm] * 7 + [vmem, smem, smem],
        out_specs=vmem,
        scratch_shapes=[
            pltpu.VMEM((GROUP, SPANS, 2, TOK, HD), bf16),
            pltpu.VMEM((GROUP, TOK, HD), bf16),
            pltpu.VMEM((GROUP, 2, 4, PART, HD), bf16),
            pltpu.VMEM((GROUP, 4, HD, GATHERED), bf16),
            pltpu.VMEM((GROUP, HD, DIRECT), bf16),
            pltpu.VMEM((PART, WIDTH), bf16),
            pltpu.VMEM((GROUP, TOK, HD), bf16),
            pltpu.VMEM((GROUP, 4, PART, HD), bf16),
            pltpu.VMEM((3, PART, DIRECT), bf16),
            pltpu.VMEM((3, PART, DIRECT), bf16),
            pltpu.VMEM((PART, WIDTH), f32),
            pltpu.VMEM((HD, TOK), f32),
            pltpu.VMEM((1, TOK), f32),
            pltpu.VMEM((1, TOK), f32),
            dma((GROUP, 16)),
            dma((GROUP, SPANS)),
            dma((GROUP, 3, 5)),
            dma((GROUP, 3, 5)),
            dma((GROUP, 3)),
            dma((GROUP, 3)),
            dma((GROUP, 8)),
            dma((GROUP, 8)),
            dma((GROUP, 3)),
            dma((GROUP, 3)),
            dma((3,)),
            dma((3,)),
            dma((8,)),
        ],
        compiler_params=pltpu.CompilerParams(
            collective_id=0, has_side_effects=True, vmem_limit_bytes=60 * 2**20
        ),
    )(q, k, v, ck, cv, hidden, weight, gate, mask, prefix)


def body(
    queries,
    keys,
    values,
    ctx_keys,
    ctx_values,
    hidden,
    out_weight,
    gates,
    levels,
    span_mask,
    prefix,
):
    span_index = lax.axis_index("tm")
    q, k, v = (a[0, 0].transpose(1, 0, 2) for a in (queries, keys, values))
    ck, cv = (a[0].transpose(1, 0, 2) for a in (ctx_keys, ctx_values))
    level_now = lax.dynamic_index_in_dim(levels, span_index, 0, keepdims=False)
    gate_row = lax.dynamic_index_in_dim(gates, level_now, 0, keepdims=True)
    weight = out_weight.reshape(GROUP, HD, WIDTH)
    updated = sublayer(q, k, v, ck, cv, hidden[0, 0], weight, gate_row, span_mask, prefix)
    return updated[None, None]


def solution(mesh):
    return jax.shard_map(
        body,
        mesh=mesh,
        in_specs=(
            P("branch", "tm", "head", None, None),
            P("branch", "tm", "head", None, None),
            P("branch", "tm", "head", None, None),
            P("tm", ("head", "branch"), None, None),
            P("tm", ("head", "branch"), None, None),
            P("branch", "tm", "head", None),
            P("head", None),
            P(),
            P(),
            P(),
            P(),
        ),
        out_specs=P("branch", "tm", "head", None),
        check_vma=False,
    )
```

```python
import math

import jax
import jax.numpy as jnp
from jax import lax
from jax.experimental import pallas as pl
from jax.experimental.pallas import tpu as pltpu
from jax.sharding import PartitionSpec as P

MESH = pl.DeviceIdType.MESH
PLANE = 8
TOK = 512
PART = 128
CHUNK = 32
HD = 128
GROUP = 5
WIDTH = 5120
GATHERED = 2560
DIRECT = WIDTH - GATHERED
TILE = 512
LOW = -1e30
EXP_SCALE = math.log2(math.e) / math.sqrt(HD)


def remote(src, dst, send_sem, recv_sem, where):
    return pltpu.make_async_remote_copy(
        src_ref=src,
        dst_ref=dst,
        send_sem=send_sem,
        recv_sem=recv_sem,
        device_id=where,
        device_id_type=MESH,
    )


def sublayer_kernel(
    q_ref,
    k_ref,
    v_ref,
    ck_ref,
    cv_ref,
    hidden_ref,
    w_ref,
    gate_ref,
    mask_ref,
    prefix_ref,
    out_ref,
    kvbuf,
    qbuf,
    ctxbuf,
    wbuf,
    wdirect,
    hbuf,
    attloc,
    attbuf,
    psend,
    precv,
    outacc,
    acc,
    stats,
    queries_in,
    far_acc,
    far_stats,
    result_out,
    result_in,
    stats_in,
    q_send,
    q_recv,
    back_send,
    back_recv,
    kv_send,
    kv_recv,
    in_send,
    in_recv,
    ctx_send,
    ctx_recv,
    w_send,
    w_recv,
    att_send,
    att_recv,
    part_send,
    part_recv,
    local,
):
    span = lax.axis_index("tm")
    x = lax.axis_index("head")
    b = lax.axis_index("branch")
    zhi = span // 8
    y = (span % 8) // 2
    core = span % 2
    place = span % 8
    lower, upper = zhi == 0, zhi == 1
    sibling = {"tm": span + 1 - 2 * core}
    across = {"tm": (span + 8) % 16}

    def at_y(step):
        return zhi * 8 + ((y + step) % 4) * 2 + core

    def at_x(step):
        return (x + step) % 4

    def rows(index, size):
        return pl.ds(pl.multiple_of(index * size, size), size)

    own_rows = rows(x, PART)

    own = pl.ds(GROUP * x, GROUP)
    home = [
        pltpu.make_async_copy(ck_ref.at[own], ctxbuf.at[:, 0, x, rows(b, CHUNK)], local.at[0]),
        pltpu.make_async_copy(cv_ref.at[own], ctxbuf.at[:, 1, x, rows(b, CHUNK)], local.at[1]),
        pltpu.make_async_copy(k_ref.at[own], kvbuf.at[:, place, 0, own_rows], local.at[2]),
        pltpu.make_async_copy(v_ref.at[own], kvbuf.at[:, place, 1, own_rows], local.at[3]),
        pltpu.make_async_copy(q_ref.at[own], qbuf.at[:, own_rows], local.at[4]),
    ]
    late = [
        pltpu.make_async_copy(w_ref.at[:, :, pl.ds(GATHERED, DIRECT)], wdirect, local.at[5]),
        pltpu.make_async_copy(w_ref.at[:, :, pl.ds(0, GATHERED)], wbuf.at[:, x], local.at[6]),
        pltpu.make_async_copy(hidden_ref, hbuf, local.at[7]),
    ]
    for copy in home:
        copy.start()

    barrier = pltpu.get_barrier_semaphore()
    partners = [sibling, across]
    for step in (1, 2, 3):
        partners += [{"tm": at_y(step)}, {"head": at_x(step)}, {"branch": (b + step) % 4}]
    for where in partners:
        pl.semaphore_signal(barrier, inc=1, device_id=where, device_id_type=MESH)
    pl.semaphore_wait(barrier, len(partners))

    def entry(h, step, kind):
        g = at_x(step)
        row = GROUP * g + h
        src, dst = (
            (lambda: (ck_ref.at[row], ctxbuf.at[h, 0, x, rows(b, CHUNK)])),
            (lambda: (cv_ref.at[row], ctxbuf.at[h, 1, x, rows(b, CHUNK)])),
            (lambda: (k_ref.at[row], kvbuf.at[h, place, 0, own_rows])),
            (lambda: (v_ref.at[row], kvbuf.at[h, place, 1, own_rows])),
            (lambda: (q_ref.at[row], qbuf.at[h, own_rows])),
        )[kind]()
        return remote(
            src, dst, in_send.at[h, step - 1, kind], in_recv.at[h, step - 1, kind], {"head": g}
        )

    def entry_start(h, kinds):
        for kind in kinds:
            for step in (1, 2, 3):
                entry(h, step, kind).start()

    def entry_wait(h, kinds):
        for kind in kinds:
            for step in (1, 2, 3):
                entry(h, step, kind).wait_recv()

    def chunk(h, step):
        part = ctxbuf.at[h, :, :, rows(b, CHUNK)]
        return remote(
            part,
            part,
            ctx_send.at[h, step - 1],
            ctx_recv.at[h, step - 1],
            {"branch": (b + step) % 4},
        )

    def spread_context(h):
        entry_wait(h, (0, 1))
        for step in (1, 2, 3):
            chunk(h, step).start()

    def item(h, c, slot, where):
        return remote(kvbuf.at[h, c], kvbuf.at[h, c], kv_send.at[h, slot], kv_recv.at[h, c], where)

    left, right = {"tm": at_y(3)}, {"tm": at_y(1)}

    def at(step):
        return ((y + step) % 4) * 2 + core

    def own_items(h):
        yield lower | (y < 3), item(h, place, 0, right)
        yield lower | (y == 0), item(h, place, 1, left)
        yield lower | (core == 0), item(h, place, 2, sibling)

    def near_arrivals(h):
        yield lower | (y > 0), item(h, at(3), 3, sibling)
        yield lower | (y == 3), item(h, at(1), 4, sibling)

    def near_items(h):
        yield from near_arrivals(h)
        back = jnp.where(upper, 3, 1 + 2 * (h % 2))
        on = lower | (y == 1) | (y == 2)
        yield on, item(h, at(back), 5, {"tm": at_y(4 - back)})

    def far_items(h):
        yield lower | (y >= 2), item(h, at(2), 6, sibling)

    def queries_across(h):
        return remote(qbuf.at[h], queries_in.at[h], q_send.at[h], q_recv.at[h], across)

    def results_back(h):
        yield remote(
            result_out.at[h], result_in.at[h], back_send.at[h, 0], back_recv.at[h, 0], across
        )
        yield remote(
            far_stats.at[h], stats_in.at[h], back_send.at[h, 1], back_recv.at[h, 1], across
        )

    def send_queries(h):
        entry_wait(h, (4,))

        @pl.when(upper)
        def _():
            queries_across(h).start()

    def send_own(h):
        for step in (1, 2, 3):
            chunk(h, step).wait_recv()
        entry_wait(h, (2, 3))
        use_context = prefix_ref[0] > span
        kvbuf[h, place] = jnp.where(
            use_context, ctxbuf[h].reshape(2, TOK, HD), kvbuf[h, place]
        )
        for cond, copy in own_items(h):
            pl.when(cond)(copy.start)

    def send_near(h):
        for cond, copy in near_arrivals(h):
            pl.when(cond)(copy.wait_recv)
        for cond, copy in reversed(list(near_items(h))):
            pl.when(cond)(copy.start)

    def send_far(h):
        for cond, copy in far_items(h):
            pl.when(cond)(copy.wait_recv)
            pl.when(cond)(copy.start)

    half = 64 * core

    def block_of_weight(h, g, start, size, slot, where, src=None):
        spot = wbuf.at[h, g, pl.ds(pl.multiple_of(start, 32), size)]
        return remote(
            spot if src is None else src, spot, w_send.at[h, slot], w_recv.at[h, slot], where
        )

    def weight_near(h, slot):
        src = w_ref.at[h, pl.ds(pl.multiple_of(half, 64), 64), pl.ds(0, GATHERED)]
        return block_of_weight(h, x, half, 64, slot, {"head": at_x((1, 3)[slot])}, src)

    def weight_far(h, slot):
        g, to = ((at_x(3), at_x(1)), (at_x(1), at_x(3)))[slot - 2]
        return block_of_weight(h, g, half + 32 * (slot - 2), 32, slot, {"head": to})

    def weight_pass(h, slot):
        if slot == 4:
            return block_of_weight(h, at_x(3), half, 64, slot, sibling)
        if slot == 5:
            return block_of_weight(h, at_x(1), half, 64, slot, sibling)
        return block_of_weight(h, at_x(2), half + 32 * (slot - 6), 32, slot, sibling)

    def start_weight(h):
        for slot in (0, 1):
            weight_near(h, slot).start()

    def relay_weight(h):
        for slot in (0, 1):
            weight_near(h, slot).wait_recv()
            weight_far(h, 2 + slot).start()
            weight_pass(h, 4 + slot).start()

    def pass_weight(h):
        for slot in (2, 3):
            weight_far(h, slot).wait_recv()
            weight_pass(h, 4 + slot).start()

    def wait_weight(h):
        for slot in (4, 5, 6, 7):
            weight_pass(h, slot).wait_recv()

    def features(h, step):
        g = at_x(step)
        return remote(
            attloc.at[h, rows(g, PART)],
            attbuf.at[h, x],
            att_send.at[h, step - 1],
            att_recv.at[h, step - 1],
            {"head": g},
        )

    def partial_sum(step):
        return remote(
            psend.at[step - 1],
            precv.at[step - 1],
            part_send.at[step - 1],
            part_recv.at[step - 1],
            {"head": at_x(step)},
        )

    def fold(h, c, query, row, total, state):
        allowed = mask_ref[row, 8 * zhi + c].astype(jnp.float32)
        s = lax.dot_general(
            kvbuf[h, c, 0], query[h], (((1,), (1,)), ((), ())), preferred_element_type=jnp.float32
        )
        top = jnp.max(s, axis=0, keepdims=True) * allowed + (1.0 - allowed) * LOW
        old = state[h, 0:1]
        new = jnp.maximum(old, top)
        p = jnp.exp2((s - (new - (1.0 - allowed) * (2.0 * LOW))) * EXP_SCALE)
        fade = jnp.exp2((old - new) * EXP_SCALE)
        state[h, 0:1] = new
        state[h, 1:2] = state[h, 1:2] * fade + jnp.sum(p, axis=0, keepdims=True)
        total[...] = total[...] * fade + lax.dot_general(
            kvbuf[h, c, 1],
            p.astype(jnp.bfloat16),
            (((0,), (0,)), ((), ())),
            preferred_element_type=jnp.float32,
        )

    def clear(h, total, state):
        total[...] = jnp.zeros_like(total)
        state[h, 0:1] = jnp.full((1, TOK), LOW, jnp.float32)
        state[h, 1:2] = jnp.zeros((1, TOK), jnp.float32)

    def compute(h):
        own_acc = acc.at[h]
        clear(h, own_acc, stats)

        @pl.when(lower)
        def _():
            clear(h, far_acc, far_stats)
            far_stats[h, 2:8] = jnp.zeros((6, TOK), jnp.float32)
            queries_across(h).wait_recv()

        def visit(i, _):
            j = i // 2
            turn = i % 2
            step = j + j // 2 - 2 * (j // 3)
            there = (y + step) % 4
            c = there * 2 + (core + turn) % 2
            seen = (there < y) | ((step == 0) & ((turn == 0) | (core == 1)))

            @pl.when((seen | lower) & (turn == 1))
            def _():
                item(h, c, 0, sibling).wait_recv()

            @pl.when(lower)
            def _():
                fold(h, c, queries_in, span + 8 * (1 - zhi), far_acc, far_stats)

            @pl.when(seen)
            def _():
                fold(h, c, qbuf, span, own_acc, stats)

            return 0

        lax.fori_loop(0, 6, visit, 0)
        send_far(h)
        lax.fori_loop(6, 8, visit, 0)

        @pl.when(lower)
        def _():
            result_out[h] = (far_acc[...] / far_stats[h, 1:2]).astype(jnp.bfloat16)
            for copy in results_back(h):
                copy.start()

    def finalize(h):
        @pl.when(lower)
        def _():
            attloc[h] = (acc[h] / stats[h, 1:2]).T.astype(jnp.bfloat16)

        @pl.when(upper)
        def _():
            for copy in results_back(h):
                copy.wait_recv()
            here, there = stats[h, 0:1], stats_in[h, 0:1]
            top = jnp.maximum(here, there)
            here, there = jnp.exp2((here - top) * EXP_SCALE), jnp.exp2((there - top) * EXP_SCALE)
            there = there * stats_in[h, 1:2]
            total = acc[h] * here + result_in[h].astype(jnp.float32) * there
            total = total / (stats[h, 1:2] * here + there)
            attloc[h] = total.T.astype(jnp.bfloat16)

        for step in (1, 2, 3):
            features(h, step).start()
        attbuf[h, x] = attloc[h, own_rows]

    def for_heads(function):
        def step(h, _):
            function(h)
            return 0

        lax.fori_loop(0, GROUP, step, 0)

    for_heads(lambda h: entry_start(h, (0, 1)))
    for_heads(lambda h: entry_start(h, (2, 3, 4)))
    for copy in late:
        copy.start()
    for copy in home:
        copy.wait()
    spread_context(0)
    spread_context(1)
    send_own(0)
    spread_context(2)
    send_queries(0)
    send_own(1)
    spread_context(3)
    start_weight(0)
    send_near(0)

    def per_head(h, _):
        @pl.when(h + 1 < GROUP)
        def _():
            send_queries(h + 1)
            send_near(h + 1)
            start_weight(h + 1)

        @pl.when(h + 2 < GROUP)
        def _():
            send_own(h + 2)

        @pl.when(h + 4 < GROUP)
        def _():
            spread_context(h + 4)

        compute(h)

        @pl.when(h >= 1)
        def _():
            finalize(h - 1)
            relay_weight(h - 1)

        @pl.when(h >= 2)
        def _():
            pass_weight(h - 2)

        return 0

    lax.fori_loop(0, GROUP, per_head, 0)
    finalize(GROUP - 1)
    relay_weight(GROUP - 1)

    late[0].wait()

    def partial_of(step):
        here = rows(at_x(step), PART)
        group = jnp.concatenate([attloc[h, here] for h in range(GROUP)], axis=1)
        for n in range(DIRECT // TILE):
            cols = slice(n * TILE, (n + 1) * TILE)
            value = jnp.dot(
                group,
                wdirect[:, :, cols].reshape(GROUP * HD, TILE),
                preferred_element_type=jnp.float32,
            )
            if step:
                psend[step - 1, :, cols] = value.astype(jnp.bfloat16)
            else:
                outacc[:, GATHERED + n * TILE : GATHERED + (n + 1) * TILE] = value

    for step in (2, 1, 3):
        partial_of(step)
        partial_sum(step).start()
    partial_of(0)
    pass_weight(GROUP - 2)
    late[1].wait()
    outacc[:, :GATHERED] = jnp.zeros((PART, GATHERED), jnp.float32)

    def project(h):
        wait_weight(h)
        for step in (1, 2, 3):
            features(h, step).wait_recv()
        group = jnp.concatenate([attbuf[h, g] for g in range(4)], axis=1)
        for n in range(GATHERED // TILE):
            cols = slice(n * TILE, (n + 1) * TILE)
            outacc[:, cols] += jnp.dot(
                group,
                wbuf[h, :, :, cols].reshape(4 * HD, TILE),
                preferred_element_type=jnp.float32,
            )

    def project_early(h, _):
        project(h)
        return 0

    lax.fori_loop(0, GROUP - 1, project_early, 0)
    pass_weight(GROUP - 1)
    project(GROUP - 1)
    late[2].wait()

    def finish(cols, projected):
        out_ref[:, cols] = (
            hbuf[:, cols].astype(jnp.float32) + gate_ref[:, cols] * projected
        ).astype(jnp.bfloat16)

    for n in range(GATHERED // TILE):
        cols = slice(n * TILE, (n + 1) * TILE)
        finish(cols, outacc[:, cols])
    for step in (1, 2, 3):
        partial_sum(step).wait_recv()
    for n in range(DIRECT // TILE):
        cols = slice(GATHERED + n * TILE, GATHERED + (n + 1) * TILE)
        there = slice(n * TILE, (n + 1) * TILE)
        total = outacc[:, cols]
        for step in (1, 2, 3):
            total += precv[step - 1, :, there].astype(jnp.float32)
        finish(cols, total)

    def sent(h):
        for step in (1, 2, 3):
            for kind in range(5):
                entry(h, step, kind).wait_send()
            chunk(h, step).wait_send()
            features(h, step).wait_send()
        for slot in (0, 1):
            weight_near(h, slot).wait_send()
        for slot in (2, 3):
            weight_far(h, slot).wait_send()
        for slot in (4, 5, 6, 7):
            weight_pass(h, slot).wait_send()
        @pl.when(upper)
        def _():
            queries_across(h).wait_send()

        @pl.when(lower)
        def _():
            for copy in results_back(h):
                copy.wait_send()

        for items in (own_items, near_items, far_items):
            for cond, copy in items(h):
                pl.when(cond)(copy.wait_send)

    for_heads(sent)
    for step in (1, 2, 3):
        partial_sum(step).wait_send()


def sublayer(q, k, v, ck, cv, hidden, weight, gate, mask, prefix):
    hbm = pl.BlockSpec(memory_space=pl.ANY)
    vmem = pl.BlockSpec(memory_space=pltpu.VMEM)
    smem = pl.BlockSpec(memory_space=pltpu.SMEM)
    bf16, f32, dma = jnp.bfloat16, jnp.float32, pltpu.SemaphoreType.DMA
    return pl.pallas_call(
        sublayer_kernel,
        out_shape=jax.ShapeDtypeStruct((PART, WIDTH), bf16),
        in_specs=[hbm] * 7 + [vmem, smem, smem],
        out_specs=vmem,
        scratch_shapes=[
            pltpu.VMEM((GROUP, PLANE, 2, TOK, HD), bf16),
            pltpu.VMEM((GROUP, TOK, HD), bf16),
            pltpu.VMEM((GROUP, 2, 4, PART, HD), bf16),
            pltpu.VMEM((GROUP, 4, HD, GATHERED), bf16),
            pltpu.VMEM((GROUP, HD, DIRECT), bf16),
            pltpu.VMEM((PART, WIDTH), bf16),
            pltpu.VMEM((GROUP, TOK, HD), bf16),
            pltpu.VMEM((GROUP, 4, PART, HD), bf16),
            pltpu.VMEM((3, PART, DIRECT), bf16),
            pltpu.VMEM((3, PART, DIRECT), bf16),
            pltpu.VMEM((PART, WIDTH), f32),
            pltpu.VMEM((GROUP, HD, TOK), f32),
            pltpu.VMEM((GROUP, 8, TOK), f32),
            pltpu.VMEM((GROUP, TOK, HD), bf16),
            pltpu.VMEM((HD, TOK), f32),
            pltpu.VMEM((GROUP, 8, TOK), f32),
            pltpu.VMEM((GROUP, HD, TOK), bf16),
            pltpu.VMEM((GROUP, HD, TOK), bf16),
            pltpu.VMEM((GROUP, 8, TOK), f32),
            dma((GROUP,)),
            dma((GROUP,)),
            dma((GROUP, 2)),
            dma((GROUP, 2)),
            dma((GROUP, 8)),
            dma((GROUP, PLANE)),
            dma((GROUP, 3, 5)),
            dma((GROUP, 3, 5)),
            dma((GROUP, 3)),
            dma((GROUP, 3)),
            dma((GROUP, 8)),
            dma((GROUP, 8)),
            dma((GROUP, 3)),
            dma((GROUP, 3)),
            dma((3,)),
            dma((3,)),
            dma((8,)),
        ],
        compiler_params=pltpu.CompilerParams(
            collective_id=0, has_side_effects=True, vmem_limit_bytes=60 * 2**20
        ),
    )(q, k, v, ck, cv, hidden, weight, gate, mask, prefix)


def body(
    queries,
    keys,
    values,
    ctx_keys,
    ctx_values,
    hidden,
    out_weight,
    gates,
    levels,
    span_mask,
    prefix,
):
    span_index = lax.axis_index("tm")
    q, k, v = (a[0, 0].transpose(1, 0, 2) for a in (queries, keys, values))
    ck, cv = (a[0].transpose(1, 0, 2) for a in (ctx_keys, ctx_values))
    level_now = lax.dynamic_index_in_dim(levels, span_index, 0, keepdims=False)
    gate_row = lax.dynamic_index_in_dim(gates, level_now, 0, keepdims=True)
    weight = out_weight.reshape(GROUP, HD, WIDTH)
    updated = sublayer(q, k, v, ck, cv, hidden[0, 0], weight, gate_row, span_mask, prefix)
    return updated[None, None]


def solution(mesh):
    return jax.shard_map(
        body,
        mesh=mesh,
        in_specs=(
            P("branch", "tm", "head", None, None),
            P("branch", "tm", "head", None, None),
            P("branch", "tm", "head", None, None),
            P("tm", ("head", "branch"), None, None),
            P("tm", ("head", "branch"), None, None),
            P("branch", "tm", "head", None),
            P("head", None),
            P(),
            P(),
            P(),
            P(),
        ),
        out_specs=P("branch", "tm", "head", None),
        check_vma=False,
    )
```

```python
import math

import jax
import jax.numpy as jnp
from jax import lax
from jax.experimental import pallas as pl
from jax.experimental.pallas import tpu as pltpu
from jax.sharding import PartitionSpec as P

MESH = pl.DeviceIdType.MESH
PLANE = 8
TOK = 512
PART = 128
CHUNK = 32
HD = 128
GROUP = 5
WIDTH = 5120
GATHERED = 4096
DIRECT = WIDTH - GATHERED
TILE = 512
LOW = -1e30
EXP_SCALE = math.log2(math.e) / math.sqrt(HD)


def remote(src, dst, send_sem, recv_sem, where):
    return pltpu.make_async_remote_copy(
        src_ref=src,
        dst_ref=dst,
        send_sem=send_sem,
        recv_sem=recv_sem,
        device_id=where,
        device_id_type=MESH,
    )


def sublayer_kernel(
    q_ref,
    k_ref,
    v_ref,
    ck_ref,
    cv_ref,
    hidden_ref,
    w_ref,
    gate_ref,
    mask_ref,
    prefix_ref,
    out_ref,
    kvbuf,
    qbuf,
    ctxbuf,
    wbuf,
    wdirect,
    hbuf,
    attloc,
    attbuf,
    psend,
    precv,
    outacc,
    score,
    acc,
    stats,
    queries_in,
    far_acc,
    far_stats,
    result_out,
    result_in,
    stats_in,
    q_send,
    q_recv,
    back_send,
    back_recv,
    kv_send,
    kv_recv,
    in_send,
    in_recv,
    ctx_send,
    ctx_recv,
    w_send,
    w_recv,
    att_send,
    att_recv,
    part_send,
    part_recv,
    local,
):
    span = lax.axis_index("tm")
    x = lax.axis_index("head")
    b = lax.axis_index("branch")
    zhi = span // 8
    y = (span % 8) // 2
    core = span % 2
    place = span % 8
    lower, upper = zhi == 0, zhi == 1
    sibling = {"tm": span + 1 - 2 * core}
    across = {"tm": (span + 8) % 16}

    def at_y(step):
        return zhi * 8 + ((y + step) % 4) * 2 + core

    def at_x(step):
        return (x + step) % 4

    def rows(index, size):
        return pl.ds(pl.multiple_of(index * size, size), size)

    own_rows = rows(x, PART)

    own = pl.ds(GROUP * x, GROUP)
    home = [
        pltpu.make_async_copy(ck_ref.at[own], ctxbuf.at[:, 0, x, rows(b, CHUNK)], local.at[0]),
        pltpu.make_async_copy(cv_ref.at[own], ctxbuf.at[:, 1, x, rows(b, CHUNK)], local.at[1]),
        pltpu.make_async_copy(k_ref.at[own], kvbuf.at[:, place, 0, own_rows], local.at[2]),
        pltpu.make_async_copy(v_ref.at[own], kvbuf.at[:, place, 1, own_rows], local.at[3]),
        pltpu.make_async_copy(q_ref.at[own], qbuf.at[:, own_rows], local.at[4]),
    ]
    late = [
        pltpu.make_async_copy(w_ref.at[:, :, pl.ds(GATHERED, DIRECT)], wdirect, local.at[5]),
        pltpu.make_async_copy(w_ref.at[:, :, pl.ds(0, GATHERED)], wbuf.at[:, x], local.at[6]),
        pltpu.make_async_copy(hidden_ref, hbuf, local.at[7]),
    ]
    for copy in home:
        copy.start()

    barrier = pltpu.get_barrier_semaphore()
    partners = [sibling, across]
    for step in (1, 2, 3):
        partners += [{"tm": at_y(step)}, {"head": at_x(step)}, {"branch": (b + step) % 4}]
    for where in partners:
        pl.semaphore_signal(barrier, inc=1, device_id=where, device_id_type=MESH)
    pl.semaphore_wait(barrier, len(partners))

    def entry(h, step, kind):
        g = at_x(step)
        row = GROUP * g + h
        src, dst = (
            (lambda: (ck_ref.at[row], ctxbuf.at[h, 0, x, rows(b, CHUNK)])),
            (lambda: (cv_ref.at[row], ctxbuf.at[h, 1, x, rows(b, CHUNK)])),
            (lambda: (k_ref.at[row], kvbuf.at[h, place, 0, own_rows])),
            (lambda: (v_ref.at[row], kvbuf.at[h, place, 1, own_rows])),
            (lambda: (q_ref.at[row], qbuf.at[h, own_rows])),
        )[kind]()
        return remote(
            src, dst, in_send.at[h, step - 1, kind], in_recv.at[h, step - 1, kind], {"head": g}
        )

    def entry_start(h, kinds):
        for kind in kinds:
            for step in (1, 2, 3):
                entry(h, step, kind).start()

    def entry_wait(h, kinds):
        for kind in kinds:
            for step in (1, 2, 3):
                entry(h, step, kind).wait_recv()

    def chunk(h, step):
        part = ctxbuf.at[h, :, :, rows(b, CHUNK)]
        return remote(
            part,
            part,
            ctx_send.at[h, step - 1],
            ctx_recv.at[h, step - 1],
            {"branch": (b + step) % 4},
        )

    def spread_context(h):
        entry_wait(h, (0, 1))
        for step in (1, 2, 3):
            chunk(h, step).start()

    def item(h, c, slot, where):
        return remote(kvbuf.at[h, c], kvbuf.at[h, c], kv_send.at[h, slot], kv_recv.at[h, c], where)

    left, right = {"tm": at_y(3)}, {"tm": at_y(1)}

    def at(step):
        return ((y + step) % 4) * 2 + core

    def own_items(h):
        yield lower | (y < 3), item(h, place, 0, right)
        yield lower | (y == 0) | ((y == 1) & (h % 2 == 1)), item(h, place, 1, left)
        yield lower | (core == 0), item(h, place, 2, sibling)

    def near_arrivals(h):
        yield lower | (y > 0), item(h, at(3), 3, sibling)
        yield lower | (y == 3), item(h, at(1), 4, sibling)

    def near_items(h):
        yield from near_arrivals(h)
        back = 3 - 2 * (h % 2)
        on = lower | (((y == 1) | (y == 2)) == (h % 2 == 0))
        yield on, item(h, at(back), 5, {"tm": at_y(4 - back)})

    def far_items(h):
        yield lower | (y >= 2), item(h, at(2), 6, sibling)

    def queries_across(h):
        return remote(qbuf.at[h], queries_in.at[h], q_send.at[h], q_recv.at[h], across)

    def results_back(h):
        yield remote(
            result_out.at[h], result_in.at[h], back_send.at[h, 0], back_recv.at[h, 0], across
        )
        yield remote(
            far_stats.at[h], stats_in.at[h], back_send.at[h, 1], back_recv.at[h, 1], across
        )

    def send_queries(h):
        entry_wait(h, (4,))

        @pl.when(upper)
        def _():
            queries_across(h).start()

    def send_own(h):
        for step in (1, 2, 3):
            chunk(h, step).wait_recv()
        entry_wait(h, (2, 3))
        use_context = prefix_ref[0] > span
        kvbuf[h, place] = jnp.where(
            use_context, ctxbuf[h].reshape(2, TOK, HD), kvbuf[h, place]
        )
        for cond, copy in own_items(h):
            pl.when(cond)(copy.start)

    def send_near(h):
        for cond, copy in near_arrivals(h):
            pl.when(cond)(copy.wait_recv)
        pl.when(upper & (y == 0) & (h % 2 == 1))(item(h, at(1), 4, sibling).wait_recv)
        for cond, copy in reversed(list(near_items(h))):
            pl.when(cond)(copy.start)

    def send_far(h):
        for cond, copy in far_items(h):
            pl.when(cond)(copy.wait_recv)
            pl.when(cond)(copy.start)

    half = 64 * core

    def pair(h):
        second = (y + h) % 2
        return half + 32 * second, {"tm": at_y(1 + 2 * second)}

    def block_of_weight(h, g, start, size, slot, where, src=None):
        spot = wbuf.at[h, g, pl.ds(pl.multiple_of(start, 16), size)]
        return remote(
            spot if src is None else src, spot, w_send.at[h, slot], w_recv.at[h, slot], where
        )

    def weight_near(h, slot):
        start, _ = pair(h)
        src = w_ref.at[h, pl.ds(pl.multiple_of(start, 32), 32), pl.ds(0, GATHERED)]
        return block_of_weight(h, x, start, 32, slot, {"head": at_x((1, 3)[slot])}, src)

    def weight_far(h, slot):
        g, to = ((at_x(3), at_x(1)), (at_x(1), at_x(3)))[slot - 2]
        return block_of_weight(h, g, pair(h)[0] + 16 * (slot - 2), 16, slot, {"head": to})

    def weight_exchange(h, slot):
        start, where = pair(h)
        return block_of_weight(h, at_x((3, 1, 2)[slot - 4]), start, 32, slot, where)

    def weight_pass(h, slot):
        return block_of_weight(h, at_x((3, 1, 2)[slot - 7]), half, 64, slot, sibling)

    def start_weight(h):
        for slot in (0, 1):
            weight_near(h, slot).start()

    def relay_weight(h):
        for slot in (0, 1):
            weight_near(h, slot).wait_recv()
            weight_far(h, 2 + slot).start()
            weight_exchange(h, 4 + slot).start()

    def pass_weight(h):
        for slot in (2, 3):
            weight_far(h, slot).wait_recv()
        weight_exchange(h, 6).start()
        for slot in (4, 5):
            weight_exchange(h, slot).wait_recv()
            weight_pass(h, 3 + slot).start()

    def last_weight(h):
        weight_exchange(h, 6).wait_recv()
        weight_pass(h, 9).start()

    def wait_weight(h):
        for slot in (7, 8, 9):
            weight_pass(h, slot).wait_recv()

    def features(h, step):
        g = at_x(step)
        return remote(
            attloc.at[h, rows(g, PART)],
            attbuf.at[h, x],
            att_send.at[h, step - 1],
            att_recv.at[h, step - 1],
            {"head": g},
        )

    def partial_sum(step):
        return remote(
            psend.at[step - 1],
            precv.at[step - 1],
            part_send.at[step - 1],
            part_recv.at[step - 1],
            {"head": at_x(step)},
        )

    def scores(h, c, query):
        return lax.dot_general(
            kvbuf[h, c, 0], query[h], (((1,), (1,)), ((), ())), preferred_element_type=jnp.float32
        )

    def fold(h, c, s, row, total, state):
        allowed = mask_ref[row, 8 * zhi + c].astype(jnp.float32)
        top = jnp.max(s, axis=0, keepdims=True) * allowed + (1.0 - allowed) * LOW
        old = state[h, 0:1]
        new = jnp.maximum(old, top)
        p = jnp.exp2((s - (new - (1.0 - allowed) * (2.0 * LOW))) * EXP_SCALE)
        fade = jnp.exp2((old - new) * EXP_SCALE)
        state[h, 0:1] = new
        state[h, 1:2] = state[h, 1:2] * fade + jnp.sum(p, axis=0, keepdims=True)
        total[...] = total[...] * fade + lax.dot_general(
            kvbuf[h, c, 1],
            p.astype(jnp.bfloat16),
            (((0,), (0,)), ((), ())),
            preferred_element_type=jnp.float32,
        )

    def clear(h, total, state):
        total[...] = jnp.zeros_like(total)
        state[h, 0:1] = jnp.full((1, TOK), LOW, jnp.float32)
        state[h, 1:2] = jnp.zeros((1, TOK), jnp.float32)

    def compute(h):
        own_acc = acc.at[h]
        far_row = span + 8 * (1 - zhi)
        clear(h, own_acc, stats)

        @pl.when(lower)
        def _():
            clear(h, far_acc, far_stats)
            far_stats[h, 2:8] = jnp.zeros((6, TOK), jnp.float32)
            queries_across(h).wait_recv()

        def where_at(i):
            j = i // 2
            turn = i % 2
            step = j + j // 2 - 2 * (j // 3)
            there = (y + step) % 4
            seen = (there < y) | ((step == 0) & ((turn == 0) | (core == 1)))
            return there * 2 + (core + turn) % 2, turn, seen

        def visit_lower(i, _):
            c, turn, _ = where_at(i)
            before, _, _ = where_at(i - 1)

            @pl.when(turn == 1)
            def _():
                item(h, c, 0, sibling).wait_recv()

            score[0] = scores(h, c, queries_in)
            fold(h, before, score[1], span, own_acc, stats)
            score[1] = scores(h, c, qbuf)
            fold(h, c, score[0], far_row, far_acc, far_stats)
            return 0

        def visit_upper(i, _):
            c, turn, seen = where_at(i)

            @pl.when(seen & (turn == 1))
            def _():
                item(h, c, 0, sibling).wait_recv()

            @pl.when(seen)
            def _():
                fold(h, c, scores(h, c, qbuf), span, own_acc, stats)

            return 0

        @pl.when(lower)
        def _():
            score[0] = scores(h, place, queries_in)
            score[1] = scores(h, place, qbuf)
            fold(h, place, score[0], far_row, far_acc, far_stats)
            lax.fori_loop(1, 6, visit_lower, 0)

        @pl.when(upper)
        def _():
            lax.fori_loop(0, 6, visit_upper, 0)

        send_far(h)

        @pl.when(lower)
        def _():
            lax.fori_loop(6, 8, visit_lower, 0)
            fold(h, where_at(7)[0], score[1], span, own_acc, stats)

        @pl.when(upper)
        def _():
            lax.fori_loop(6, 8, visit_upper, 0)

        @pl.when(lower)
        def _():
            result_out[h] = (far_acc[...] / far_stats[h, 1:2]).astype(jnp.bfloat16)
            for copy in results_back(h):
                copy.start()

    def finalize(h):
        @pl.when(lower)
        def _():
            attloc[h] = (acc[h] / stats[h, 1:2]).T.astype(jnp.bfloat16)

        @pl.when(upper)
        def _():
            for copy in results_back(h):
                copy.wait_recv()
            here, there = stats[h, 0:1], stats_in[h, 0:1]
            top = jnp.maximum(here, there)
            here, there = jnp.exp2((here - top) * EXP_SCALE), jnp.exp2((there - top) * EXP_SCALE)
            there = there * stats_in[h, 1:2]
            total = acc[h] * here + result_in[h].astype(jnp.float32) * there
            total = total / (stats[h, 1:2] * here + there)
            attloc[h] = total.T.astype(jnp.bfloat16)

        for step in (1, 2, 3):
            features(h, step).start()
        attbuf[h, x] = attloc[h, own_rows]

    def for_heads(function):
        def step(h, _):
            function(h)
            return 0

        lax.fori_loop(0, GROUP, step, 0)

    for h in (0, 1):
        entry_start(h, (0, 1, 2, 3, 4))
    for h in (2, 3, 4):
        entry_start(h, (0, 1))
    for copy in home:
        copy.wait()
    spread_context(0)
    spread_context(1)
    send_own(0)
    send_queries(0)
    entry_start(2, (2, 3, 4))
    spread_context(2)
    send_own(1)
    send_near(0)
    entry_start(3, (2, 3, 4))
    spread_context(3)
    spread_context(4)
    send_queries(1)
    send_own(2)
    entry_start(4, (2, 3, 4))
    for copy in late:
        copy.start()
    start_weight(0)
    start_weight(1)

    def per_head(h, _):
        @pl.when(h + 1 < GROUP)
        def _():
            send_near(h + 1)

        @pl.when(h + 2 < GROUP)
        def _():
            send_queries(h + 2)
            start_weight(h + 2)

        @pl.when(h + 3 < GROUP)
        def _():
            send_own(h + 3)

        compute(h)

        @pl.when(h >= 1)
        def _():
            finalize(h - 1)

        relay_weight(h)

        @pl.when(h >= 1)
        def _():
            pass_weight(h - 1)

        @pl.when(h >= 2)
        def _():
            last_weight(h - 2)

        return 0

    lax.fori_loop(0, GROUP, per_head, 0)
    finalize(GROUP - 1)

    late[0].wait()

    def partial_of(step):
        here = rows(at_x(step), PART)
        group = jnp.concatenate([attloc[h, here] for h in range(GROUP)], axis=1)
        for n in range(DIRECT // TILE):
            cols = slice(n * TILE, (n + 1) * TILE)
            value = jnp.dot(
                group,
                wdirect[:, :, cols].reshape(GROUP * HD, TILE),
                preferred_element_type=jnp.float32,
            )
            if step:
                psend[step - 1, :, cols] = value.astype(jnp.bfloat16)
            else:
                outacc[:, GATHERED + n * TILE : GATHERED + (n + 1) * TILE] = value

    for step in (2, 1, 3):
        partial_of(step)
        partial_sum(step).start()
    pass_weight(GROUP - 1)
    partial_of(0)
    last_weight(GROUP - 2)
    late[1].wait()
    outacc[:, :GATHERED] = jnp.zeros((PART, GATHERED), jnp.float32)

    def project(h):
        wait_weight(h)
        for step in (1, 2, 3):
            features(h, step).wait_recv()
        group = jnp.concatenate([attbuf[h, g] for g in range(4)], axis=1)
        for n in range(GATHERED // TILE):
            cols = slice(n * TILE, (n + 1) * TILE)
            outacc[:, cols] += jnp.dot(
                group,
                wbuf[h, :, :, cols].reshape(4 * HD, TILE),
                preferred_element_type=jnp.float32,
            )

    def project_early(h, _):
        project(h)
        return 0

    lax.fori_loop(0, GROUP - 1, project_early, 0)
    last_weight(GROUP - 1)
    project(GROUP - 1)
    late[2].wait()

    def finish(cols, projected):
        out_ref[:, cols] = (
            hbuf[:, cols].astype(jnp.float32) + gate_ref[:, cols] * projected
        ).astype(jnp.bfloat16)

    for n in range(GATHERED // TILE):
        cols = slice(n * TILE, (n + 1) * TILE)
        finish(cols, outacc[:, cols])
    for step in (1, 2, 3):
        partial_sum(step).wait_recv()
    for n in range(DIRECT // TILE):
        cols = slice(GATHERED + n * TILE, GATHERED + (n + 1) * TILE)
        there = slice(n * TILE, (n + 1) * TILE)
        total = outacc[:, cols]
        for step in (1, 2, 3):
            total += precv[step - 1, :, there].astype(jnp.float32)
        finish(cols, total)

    def sent(h):
        for step in (1, 2, 3):
            for kind in range(5):
                entry(h, step, kind).wait_send()
            chunk(h, step).wait_send()
            features(h, step).wait_send()
        for slot in (0, 1):
            weight_near(h, slot).wait_send()
        for slot in (2, 3):
            weight_far(h, slot).wait_send()
        for slot in (4, 5, 6):
            weight_exchange(h, slot).wait_send()
        for slot in (7, 8, 9):
            weight_pass(h, slot).wait_send()
        @pl.when(upper)
        def _():
            queries_across(h).wait_send()

        @pl.when(lower)
        def _():
            for copy in results_back(h):
                copy.wait_send()

        for items in (own_items, near_items, far_items):
            for cond, copy in items(h):
                pl.when(cond)(copy.wait_send)

    for_heads(sent)
    for step in (1, 2, 3):
        partial_sum(step).wait_send()


def sublayer(q, k, v, ck, cv, hidden, weight, gate, mask, prefix):
    hbm = pl.BlockSpec(memory_space=pl.ANY)
    vmem = pl.BlockSpec(memory_space=pltpu.VMEM)
    smem = pl.BlockSpec(memory_space=pltpu.SMEM)
    bf16, f32, dma = jnp.bfloat16, jnp.float32, pltpu.SemaphoreType.DMA
    return pl.pallas_call(
        sublayer_kernel,
        out_shape=jax.ShapeDtypeStruct((PART, WIDTH), bf16),
        in_specs=[hbm] * 7 + [vmem, smem, smem],
        out_specs=vmem,
        scratch_shapes=[
            pltpu.VMEM((GROUP, PLANE, 2, TOK, HD), bf16),
            pltpu.VMEM((GROUP, TOK, HD), bf16),
            pltpu.VMEM((GROUP, 2, 4, PART, HD), bf16),
            pltpu.VMEM((GROUP, 4, HD, GATHERED), bf16),
            pltpu.VMEM((GROUP, HD, DIRECT), bf16),
            pltpu.VMEM((PART, WIDTH), bf16),
            pltpu.VMEM((GROUP, TOK, HD), bf16),
            pltpu.VMEM((GROUP, 4, PART, HD), bf16),
            pltpu.VMEM((3, PART, DIRECT), bf16),
            pltpu.VMEM((3, PART, DIRECT), bf16),
            pltpu.VMEM((PART, WIDTH), f32),
            pltpu.VMEM((2, TOK, TOK), f32),
            pltpu.VMEM((GROUP, HD, TOK), f32),
            pltpu.VMEM((GROUP, 8, TOK), f32),
            pltpu.VMEM((GROUP, TOK, HD), bf16),
            pltpu.VMEM((HD, TOK), f32),
            pltpu.VMEM((GROUP, 8, TOK), f32),
            pltpu.VMEM((GROUP, HD, TOK), bf16),
            pltpu.VMEM((GROUP, HD, TOK), bf16),
            pltpu.VMEM((GROUP, 8, TOK), f32),
            dma((GROUP,)),
            dma((GROUP,)),
            dma((GROUP, 2)),
            dma((GROUP, 2)),
            dma((GROUP, 8)),
            dma((GROUP, PLANE)),
            dma((GROUP, 3, 5)),
            dma((GROUP, 3, 5)),
            dma((GROUP, 3)),
            dma((GROUP, 3)),
            dma((GROUP, 10)),
            dma((GROUP, 10)),
            dma((GROUP, 3)),
            dma((GROUP, 3)),
            dma((3,)),
            dma((3,)),
            dma((8,)),
        ],
        compiler_params=pltpu.CompilerParams(
            collective_id=0, has_side_effects=True, vmem_limit_bytes=60 * 2**20
        ),
    )(q, k, v, ck, cv, hidden, weight, gate, mask, prefix)


def body(
    queries,
    keys,
    values,
    ctx_keys,
    ctx_values,
    hidden,
    out_weight,
    gates,
    levels,
    span_mask,
    prefix,
):
    span_index = lax.axis_index("tm")
    q, k, v = (a[0, 0].transpose(1, 0, 2) for a in (queries, keys, values))
    ck, cv = (a[0].transpose(1, 0, 2) for a in (ctx_keys, ctx_values))
    level_now = lax.dynamic_index_in_dim(levels, span_index, 0, keepdims=False)
    gate_row = lax.dynamic_index_in_dim(gates, level_now, 0, keepdims=True)
    weight = out_weight.reshape(GROUP, HD, WIDTH)
    updated = sublayer(q, k, v, ck, cv, hidden[0, 0], weight, gate_row, span_mask, prefix)
    return updated[None, None]


def solution(mesh):
    return jax.shard_map(
        body,
        mesh=mesh,
        in_specs=(
            P("branch", "tm", "head", None, None),
            P("branch", "tm", "head", None, None),
            P("branch", "tm", "head", None, None),
            P("tm", ("head", "branch"), None, None),
            P("tm", ("head", "branch"), None, None),
            P("branch", "tm", "head", None),
            P("head", None),
            P(),
            P(),
            P(),
            P(),
        ),
        out_specs=P("branch", "tm", "head", None),
        check_vma=False,
    )
```

```python
import math

import jax
import jax.numpy as jnp
from jax import lax
from jax.experimental import pallas as pl
from jax.experimental.pallas import tpu as pltpu
from jax.sharding import PartitionSpec as P

MESH = pl.DeviceIdType.MESH
PLANE = 8
TOK = 512
PART = 128
CHUNK = 32
HD = 128
GROUP = 5
WIDTH = 5120
GATHERED = 4096
DIRECT = WIDTH - GATHERED
TILE = 512
LOW = -1e30
EXP_SCALE = math.log2(math.e) / math.sqrt(HD)


def remote(src, dst, send_sem, recv_sem, where):
    return pltpu.make_async_remote_copy(
        src_ref=src,
        dst_ref=dst,
        send_sem=send_sem,
        recv_sem=recv_sem,
        device_id=where,
        device_id_type=MESH,
    )


def sublayer_kernel(
    q_ref,
    k_ref,
    v_ref,
    ck_ref,
    cv_ref,
    hidden_ref,
    w_ref,
    gates_ref,
    levels_ref,
    mask_ref,
    prefix_ref,
    out_ref,
    kvbuf,
    qbuf,
    ctxbuf,
    wbuf,
    wdirect,
    hbuf,
    attloc,
    attbuf,
    psend,
    precv,
    outacc,
    score,
    acc,
    stats,
    queries_in,
    far_acc,
    far_stats,
    result_out,
    result_in,
    stats_in,
    q_send,
    q_recv,
    back_send,
    back_recv,
    kv_send,
    kv_recv,
    in_send,
    in_recv,
    ctx_send,
    ctx_recv,
    w_send,
    w_recv,
    att_send,
    att_recv,
    part_send,
    part_recv,
    local,
):
    span = lax.axis_index("tm")
    x = lax.axis_index("head")
    b = lax.axis_index("branch")
    zhi = span // 8
    y = (span % 8) // 2
    core = span % 2
    place = span % 8
    lower, upper = zhi == 0, zhi == 1
    sibling = {"tm": span + 1 - 2 * core}
    across = {"tm": (span + 8) % 16}

    def at_y(step):
        return zhi * 8 + ((y + step) % 4) * 2 + core

    def at_x(step):
        return (x + step) % 4

    def rows(index, size):
        return pl.ds(pl.multiple_of(index * size, size), size)

    own_rows = rows(x, PART)

    own = pl.ds(GROUP * x, GROUP)
    home = [
        pltpu.make_async_copy(ck_ref.at[own], ctxbuf.at[:, 0, x, rows(b, CHUNK)], local.at[0]),
        pltpu.make_async_copy(cv_ref.at[own], ctxbuf.at[:, 1, x, rows(b, CHUNK)], local.at[1]),
        pltpu.make_async_copy(k_ref.at[own], kvbuf.at[:, place, 0, own_rows], local.at[2]),
        pltpu.make_async_copy(v_ref.at[own], kvbuf.at[:, place, 1, own_rows], local.at[3]),
        pltpu.make_async_copy(q_ref.at[own], qbuf.at[:, own_rows], local.at[4]),
    ]
    late = [
        pltpu.make_async_copy(w_ref.at[:, :, pl.ds(GATHERED, DIRECT)], wdirect, local.at[5]),
        pltpu.make_async_copy(w_ref.at[:, :, pl.ds(0, GATHERED)], wbuf.at[:, x], local.at[6]),
        pltpu.make_async_copy(hidden_ref, hbuf, local.at[7]),
    ]
    for copy in home:
        copy.start()

    barrier = pltpu.get_barrier_semaphore()
    partners = [sibling, across]
    for step in (1, 2, 3):
        partners += [{"tm": at_y(step)}, {"head": at_x(step)}, {"branch": (b + step) % 4}]
    for where in partners:
        pl.semaphore_signal(barrier, inc=1, device_id=where, device_id_type=MESH)
    pl.semaphore_wait(barrier, len(partners))

    def entry(h, step, kind):
        g = at_x(step)
        row = GROUP * g + h
        src, dst = (
            (lambda: (ck_ref.at[row], ctxbuf.at[h, 0, x, rows(b, CHUNK)])),
            (lambda: (cv_ref.at[row], ctxbuf.at[h, 1, x, rows(b, CHUNK)])),
            (lambda: (k_ref.at[row], kvbuf.at[h, place, 0, own_rows])),
            (lambda: (v_ref.at[row], kvbuf.at[h, place, 1, own_rows])),
            (lambda: (q_ref.at[row], qbuf.at[h, own_rows])),
        )[kind]()
        return remote(
            src, dst, in_send.at[h, step - 1, kind], in_recv.at[h, step - 1, kind], {"head": g}
        )

    def entry_start(h, kinds):
        for kind in kinds:
            for step in (1, 2, 3):
                entry(h, step, kind).start()

    def entry_wait(h, kinds):
        for kind in kinds:
            for step in (1, 2, 3):
                entry(h, step, kind).wait_recv()

    def chunk(h, step):
        part = ctxbuf.at[h, :, :, rows(b, CHUNK)]
        return remote(
            part,
            part,
            ctx_send.at[h, step - 1],
            ctx_recv.at[h, step - 1],
            {"branch": (b + step) % 4},
        )

    def spread_context(h):
        entry_wait(h, (0, 1))
        for step in (1, 2, 3):
            chunk(h, step).start()

    def item(h, c, slot, where):
        return remote(kvbuf.at[h, c], kvbuf.at[h, c], kv_send.at[h, slot], kv_recv.at[h, c], where)

    left, right = {"tm": at_y(3)}, {"tm": at_y(1)}

    def at(step):
        return ((y + step) % 4) * 2 + core

    def own_items(h):
        yield lower | (y < 3), item(h, place, 0, right)
        yield lower | (y == 0) | ((y == 1) & (h % 2 == 1)), item(h, place, 1, left)
        yield lower | (core == 0), item(h, place, 2, sibling)

    def near_arrivals(h):
        yield lower | (y > 0), item(h, at(3), 3, sibling)
        yield lower | (y == 3), item(h, at(1), 4, sibling)

    def near_items(h):
        yield from near_arrivals(h)
        back = 3 - 2 * (h % 2)
        on = lower | (((y == 1) | (y == 2)) == (h % 2 == 0))
        yield on, item(h, at(back), 5, {"tm": at_y(4 - back)})

    def far_items(h):
        yield lower | (y >= 2), item(h, at(2), 6, sibling)

    def queries_across(h):
        return remote(qbuf.at[h], queries_in.at[h], q_send.at[h], q_recv.at[h], across)

    def results_back(h):
        yield remote(
            result_out.at[h], result_in.at[h], back_send.at[h, 0], back_recv.at[h, 0], across
        )
        yield remote(
            far_stats.at[h], stats_in.at[h], back_send.at[h, 1], back_recv.at[h, 1], across
        )

    def send_queries(h):
        entry_wait(h, (4,))

        @pl.when(upper)
        def _():
            queries_across(h).start()

    def send_own(h):
        for step in (1, 2, 3):
            chunk(h, step).wait_recv()
        entry_wait(h, (2, 3))
        use_context = prefix_ref[0] > span
        kvbuf[h, place] = jnp.where(
            use_context, ctxbuf[h].reshape(2, TOK, HD), kvbuf[h, place]
        )
        for cond, copy in own_items(h):
            pl.when(cond)(copy.start)

    def send_near(h):
        for cond, copy in near_arrivals(h):
            pl.when(cond)(copy.wait_recv)
        pl.when(upper & (y == 0) & (h % 2 == 1))(item(h, at(1), 4, sibling).wait_recv)
        for cond, copy in reversed(list(near_items(h))):
            pl.when(cond)(copy.start)

    def send_far(h):
        for cond, copy in far_items(h):
            pl.when(cond)(copy.wait_recv)
            pl.when(cond)(copy.start)

    half = 64 * core

    def pair(h):
        second = (y + h) % 2
        return half + 32 * second, {"tm": at_y(1 + 2 * second)}

    def block_of_weight(h, g, start, size, slot, where, src=None):
        spot = wbuf.at[h, g, pl.ds(pl.multiple_of(start, 16), size)]
        return remote(
            spot if src is None else src, spot, w_send.at[h, slot], w_recv.at[h, slot], where
        )

    def weight_near(h, slot):
        start, _ = pair(h)
        src = w_ref.at[h, pl.ds(pl.multiple_of(start, 32), 32), pl.ds(0, GATHERED)]
        return block_of_weight(h, x, start, 32, slot, {"head": at_x((1, 3)[slot])}, src)

    def weight_far(h, slot):
        g, to = ((at_x(3), at_x(1)), (at_x(1), at_x(3)))[slot - 2]
        return block_of_weight(h, g, pair(h)[0] + 16 * (slot - 2), 16, slot, {"head": to})

    def weight_exchange(h, slot):
        start, where = pair(h)
        return block_of_weight(h, at_x((3, 1, 2)[slot - 4]), start, 32, slot, where)

    def weight_pass(h, slot):
        return block_of_weight(h, at_x((3, 1, 2)[slot - 7]), half, 64, slot, sibling)

    def start_weight(h):
        for slot in (0, 1):
            weight_near(h, slot).start()

    def relay_weight(h):
        for slot in (0, 1):
            weight_near(h, slot).wait_recv()
            weight_far(h, 2 + slot).start()
            weight_exchange(h, 4 + slot).start()

    def pass_weight(h):
        for slot in (2, 3):
            weight_far(h, slot).wait_recv()
        weight_exchange(h, 6).start()
        for slot in (4, 5):
            weight_exchange(h, slot).wait_recv()
            weight_pass(h, 3 + slot).start()

    def last_weight(h):
        weight_exchange(h, 6).wait_recv()
        weight_pass(h, 9).start()

    def wait_weight(h):
        for slot in (7, 8, 9):
            weight_pass(h, slot).wait_recv()

    def features(h, step):
        g = at_x(step)
        return remote(
            attloc.at[h, rows(g, PART)],
            attbuf.at[h, x],
            att_send.at[h, step - 1],
            att_recv.at[h, step - 1],
            {"head": g},
        )

    def partial_sum(step):
        return remote(
            psend.at[step - 1],
            precv.at[step - 1],
            part_send.at[step - 1],
            part_recv.at[step - 1],
            {"head": at_x(step)},
        )

    def scores(h, c, query):
        return lax.dot_general(
            kvbuf[h, c, 0], query[h], (((1,), (1,)), ((), ())), preferred_element_type=jnp.float32
        )

    def fold(h, c, s, row, total, state):
        allowed = mask_ref[row, 8 * zhi + c].astype(jnp.float32)
        top = jnp.max(s, axis=0, keepdims=True) * allowed + (1.0 - allowed) * LOW
        old = state[h, 0:1]
        new = jnp.maximum(old, top)
        p = jnp.exp2((s - (new - (1.0 - allowed) * (2.0 * LOW))) * EXP_SCALE)
        fade = jnp.exp2((old - new) * EXP_SCALE)
        state[h, 0:1] = new
        state[h, 1:2] = state[h, 1:2] * fade + jnp.sum(p, axis=0, keepdims=True)
        total[...] = total[...] * fade + lax.dot_general(
            kvbuf[h, c, 1],
            p.astype(jnp.bfloat16),
            (((0,), (0,)), ((), ())),
            preferred_element_type=jnp.float32,
        )

    def clear(h, total, state):
        total[...] = jnp.zeros_like(total)
        state[h, 0:1] = jnp.full((1, TOK), LOW, jnp.float32)
        state[h, 1:2] = jnp.zeros((1, TOK), jnp.float32)

    def compute(h):
        own_acc = acc.at[h]
        far_row = span + 8 * (1 - zhi)
        clear(h, own_acc, stats)

        @pl.when(lower)
        def _():
            clear(h, far_acc, far_stats)
            far_stats[h, 2:8] = jnp.zeros((6, TOK), jnp.float32)
            queries_across(h).wait_recv()

        def where_at(i):
            j = i // 2
            turn = i % 2
            step = j + j // 2 - 2 * (j // 3)
            there = (y + step) % 4
            seen = (there < y) | ((step == 0) & ((turn == 0) | (core == 1)))
            return there * 2 + (core + turn) % 2, turn, seen

        def visit_lower(i, _):
            c, turn, _ = where_at(i)
            before, _, _ = where_at(i - 1)

            @pl.when(turn == 1)
            def _():
                item(h, c, 0, sibling).wait_recv()

            score[0] = scores(h, c, queries_in)
            fold(h, before, score[1], span, own_acc, stats)
            score[1] = scores(h, c, qbuf)
            fold(h, c, score[0], far_row, far_acc, far_stats)
            return 0

        def visit_upper(i, _):
            c, turn, seen = where_at(i)

            @pl.when(seen & (turn == 1))
            def _():
                item(h, c, 0, sibling).wait_recv()

            @pl.when(seen)
            def _():
                fold(h, c, scores(h, c, qbuf), span, own_acc, stats)

            return 0

        @pl.when(lower)
        def _():
            score[0] = scores(h, place, queries_in)
            score[1] = scores(h, place, qbuf)
            fold(h, place, score[0], far_row, far_acc, far_stats)
            lax.fori_loop(1, 6, visit_lower, 0)

        @pl.when(upper)
        def _():
            lax.fori_loop(0, 6, visit_upper, 0)

        send_far(h)

        @pl.when(lower)
        def _():
            lax.fori_loop(6, 8, visit_lower, 0)
            fold(h, where_at(7)[0], score[1], span, own_acc, stats)

        @pl.when(upper)
        def _():
            lax.fori_loop(6, 8, visit_upper, 0)

        @pl.when(lower)
        def _():
            result_out[h] = (far_acc[...] / far_stats[h, 1:2]).astype(jnp.bfloat16)
            for copy in results_back(h):
                copy.start()

    def finalize(h):
        @pl.when(lower)
        def _():
            attloc[h] = (acc[h] / stats[h, 1:2]).T.astype(jnp.bfloat16)

        @pl.when(upper)
        def _():
            for copy in results_back(h):
                copy.wait_recv()
            here, there = stats[h, 0:1], stats_in[h, 0:1]
            top = jnp.maximum(here, there)
            here, there = jnp.exp2((here - top) * EXP_SCALE), jnp.exp2((there - top) * EXP_SCALE)
            there = there * stats_in[h, 1:2]
            total = acc[h] * here + result_in[h].astype(jnp.float32) * there
            total = total / (stats[h, 1:2] * here + there)
            attloc[h] = total.T.astype(jnp.bfloat16)

        for step in (1, 2, 3):
            features(h, step).start()
        attbuf[h, x] = attloc[h, own_rows]

    def for_heads(function):
        def step(h, _):
            function(h)
            return 0

        lax.fori_loop(0, GROUP, step, 0)

    for h in (0, 1):
        entry_start(h, (0, 1, 2, 3, 4))
    for h in (2, 3, 4):
        entry_start(h, (0, 1))
    for copy in home:
        copy.wait()
    spread_context(0)
    spread_context(1)
    send_own(0)
    send_queries(0)
    entry_start(2, (2, 3, 4))
    spread_context(2)
    send_own(1)
    send_near(0)
    entry_start(3, (2, 3, 4))
    spread_context(3)
    spread_context(4)
    send_queries(1)
    send_own(2)
    entry_start(4, (2, 3, 4))
    for copy in late:
        copy.start()
    start_weight(0)
    start_weight(1)

    def per_head(h, _):
        @pl.when(h + 1 < GROUP)
        def _():
            send_near(h + 1)

        @pl.when(h + 2 < GROUP)
        def _():
            send_queries(h + 2)
            start_weight(h + 2)

        @pl.when(h + 3 < GROUP)
        def _():
            send_own(h + 3)

        compute(h)

        @pl.when(h >= 1)
        def _():
            finalize(h - 1)

        relay_weight(h)

        @pl.when(h >= 1)
        def _():
            pass_weight(h - 1)

        @pl.when(h >= 2)
        def _():
            last_weight(h - 2)

        return 0

    lax.fori_loop(0, GROUP, per_head, 0)
    finalize(GROUP - 1)

    late[0].wait()

    def partial_of(step):
        here = rows(at_x(step), PART)
        group = jnp.concatenate([attloc[h, here] for h in range(GROUP)], axis=1)
        for n in range(DIRECT // TILE):
            cols = slice(n * TILE, (n + 1) * TILE)
            value = jnp.dot(
                group,
                wdirect[:, :, cols].reshape(GROUP * HD, TILE),
                preferred_element_type=jnp.float32,
            )
            if step:
                psend[step - 1, :, cols] = value.astype(jnp.bfloat16)
            else:
                outacc[:, GATHERED + n * TILE : GATHERED + (n + 1) * TILE] = value

    for step in (2, 1, 3):
        partial_of(step)
        partial_sum(step).start()
    pass_weight(GROUP - 1)
    partial_of(0)
    last_weight(GROUP - 2)
    late[1].wait()
    outacc[:, :GATHERED] = jnp.zeros((PART, GATHERED), jnp.float32)

    def project(h):
        wait_weight(h)
        for step in (1, 2, 3):
            features(h, step).wait_recv()
        group = jnp.concatenate([attbuf[h, g] for g in range(4)], axis=1)
        for n in range(GATHERED // TILE):
            cols = slice(n * TILE, (n + 1) * TILE)
            outacc[:, cols] += jnp.dot(
                group,
                wbuf[h, :, :, cols].reshape(4 * HD, TILE),
                preferred_element_type=jnp.float32,
            )

    def project_early(h, _):
        project(h)
        return 0

    lax.fori_loop(0, GROUP - 1, project_early, 0)
    last_weight(GROUP - 1)
    project(GROUP - 1)
    late[2].wait()

    def finish(cols, projected):
        out_ref[:, cols] = (
            hbuf[:, cols].astype(jnp.float32) + gates_ref[pl.ds(levels_ref[span], 1), cols] * projected
        ).astype(jnp.bfloat16)

    for n in range(GATHERED // TILE):
        cols = slice(n * TILE, (n + 1) * TILE)
        finish(cols, outacc[:, cols])
    for step in (1, 2, 3):
        partial_sum(step).wait_recv()
    for n in range(DIRECT // TILE):
        cols = slice(GATHERED + n * TILE, GATHERED + (n + 1) * TILE)
        there = slice(n * TILE, (n + 1) * TILE)
        total = outacc[:, cols]
        for step in (1, 2, 3):
            total += precv[step - 1, :, there].astype(jnp.float32)
        finish(cols, total)

    def sent(h):
        for step in (1, 2, 3):
            for kind in range(5):
                entry(h, step, kind).wait_send()
            chunk(h, step).wait_send()
            features(h, step).wait_send()
        for slot in (0, 1):
            weight_near(h, slot).wait_send()
        for slot in (2, 3):
            weight_far(h, slot).wait_send()
        for slot in (4, 5, 6):
            weight_exchange(h, slot).wait_send()
        for slot in (7, 8, 9):
            weight_pass(h, slot).wait_send()
        @pl.when(upper)
        def _():
            queries_across(h).wait_send()

        @pl.when(lower)
        def _():
            for copy in results_back(h):
                copy.wait_send()

        for items in (own_items, near_items, far_items):
            for cond, copy in items(h):
                pl.when(cond)(copy.wait_send)

    for_heads(sent)
    for step in (1, 2, 3):
        partial_sum(step).wait_send()


def sublayer(q, k, v, ck, cv, hidden, weight, gates, levels, mask, prefix):
    hbm = pl.BlockSpec(memory_space=pl.ANY)
    vmem = pl.BlockSpec(memory_space=pltpu.VMEM)
    smem = pl.BlockSpec(memory_space=pltpu.SMEM)
    bf16, f32, dma = jnp.bfloat16, jnp.float32, pltpu.SemaphoreType.DMA
    return pl.pallas_call(
        sublayer_kernel,
        out_shape=jax.ShapeDtypeStruct((PART, WIDTH), bf16),
        in_specs=[hbm] * 7 + [vmem, smem, smem, smem],
        out_specs=vmem,
        scratch_shapes=[
            pltpu.VMEM((GROUP, PLANE, 2, TOK, HD), bf16),
            pltpu.VMEM((GROUP, TOK, HD), bf16),
            pltpu.VMEM((GROUP, 2, 4, PART, HD), bf16),
            pltpu.VMEM((GROUP, 4, HD, GATHERED), bf16),
            pltpu.VMEM((GROUP, HD, DIRECT), bf16),
            pltpu.VMEM((PART, WIDTH), bf16),
            pltpu.VMEM((GROUP, TOK, HD), bf16),
            pltpu.VMEM((GROUP, 4, PART, HD), bf16),
            pltpu.VMEM((3, PART, DIRECT), bf16),
            pltpu.VMEM((3, PART, DIRECT), bf16),
            pltpu.VMEM((PART, WIDTH), f32),
            pltpu.VMEM((2, TOK, TOK), f32),
            pltpu.VMEM((GROUP, HD, TOK), f32),
            pltpu.VMEM((GROUP, 8, TOK), f32),
            pltpu.VMEM((GROUP, TOK, HD), bf16),
            pltpu.VMEM((HD, TOK), f32),
            pltpu.VMEM((GROUP, 8, TOK), f32),
            pltpu.VMEM((GROUP, HD, TOK), bf16),
            pltpu.VMEM((GROUP, HD, TOK), bf16),
            pltpu.VMEM((GROUP, 8, TOK), f32),
            dma((GROUP,)),
            dma((GROUP,)),
            dma((GROUP, 2)),
            dma((GROUP, 2)),
            dma((GROUP, 8)),
            dma((GROUP, PLANE)),
            dma((GROUP, 3, 5)),
            dma((GROUP, 3, 5)),
            dma((GROUP, 3)),
            dma((GROUP, 3)),
            dma((GROUP, 10)),
            dma((GROUP, 10)),
            dma((GROUP, 3)),
            dma((GROUP, 3)),
            dma((3,)),
            dma((3,)),
            dma((8,)),
        ],
        compiler_params=pltpu.CompilerParams(
            collective_id=0, has_side_effects=True, vmem_limit_bytes=60 * 2**20
        ),
    )(q, k, v, ck, cv, hidden, weight, gates, levels, mask, prefix)


def body(
    queries,
    keys,
    values,
    ctx_keys,
    ctx_values,
    hidden,
    out_weight,
    gates,
    levels,
    span_mask,
    prefix,
):
    q, k, v = (a[0, 0].transpose(1, 0, 2) for a in (queries, keys, values))
    ck, cv = (a[0].transpose(1, 0, 2) for a in (ctx_keys, ctx_values))
    weight = out_weight.reshape(GROUP, HD, WIDTH)
    updated = sublayer(
        q, k, v, ck, cv, hidden[0, 0], weight, gates, levels, span_mask, prefix
    )
    return updated[None, None]


def solution(mesh):
    return jax.shard_map(
        body,
        mesh=mesh,
        in_specs=(
            P("branch", "tm", "head", None, None),
            P("branch", "tm", "head", None, None),
            P("branch", "tm", "head", None, None),
            P("tm", ("head", "branch"), None, None),
            P("tm", ("head", "branch"), None, None),
            P("branch", "tm", "head", None),
            P("head", None),
            P(),
            P(),
            P(),
            P(),
        ),
        out_specs=P("branch", "tm", "head", None),
        check_vma=False,
    )
```
